32 devices in a mesh: grp: 4 (over y, x), dev: 8 (over z, core).
Axes of the slice: x: 2, y: 2, z: 4, core: 2. Of those that a mesh axis runs over, the one named last changes fastest.
Arguments:
- border: bfloat16 [4, 131072, 1024], P('grp', 'dev'), may hold values from -1.5 to 1.5
- inverse_blocks: bfloat16 [4, 1024, 1024], P('grp')
- selected: int32 [256], replicated, may hold values from 0 to 131071, as said below
- assignment: int32 [4], replicated, may hold values from 0 to 3, each once
- probability: float32 [4], replicated, may hold values from 2 to 8
- prior_panel: bfloat16 [131072, 256], P(('dev', 'grp'))
Outputs:
- panel_out: float32 [131072, 256], P(('dev', 'grp'))
- residual: float32 [4, 1024, 256], P('grp', 'dev')
The draws below stay inside these ranges and needn't reach their ends.
Inputs may be any that keep to these rules, and one draw needn't show every extreme that they name: `selected`: 256 distinct rows.
All inputs are finite; a program needn't handle non-finite values.
Results may differ from the reference program's by a relative error of at most 0.0005.
The reference program's roundings to bfloat16 on the way (of `picked`, `project` and `rounded`) count: a program that leaves them out, or rounds other values in their place, can miss the bound.
Values may be sent and summed in bfloat16 or wider, within the bound.
No kernel may reach another device: no remote copies, remote signals or barrier semaphores. Data moves between devices by JAX's collectives and lax.ppermute only.
A program may use at most 128 MiB of HBM per device.

```python
import math
import jax
import jax.numpy as jnp
from jax import lax

N1 = 131072
E = 1024
W = 256
GROUPS = 4


def choose_rows(key):
    order = jax.random.permutation(jax.random.fold_in(key, 11), N1)
    return order[:W].astype(jnp.int32)


def draw_selected(key, part):
    return choose_rows(key)


def draw_prior_panel(key, part):
    rows_taken = choose_rows(key)
    values = jax.random.normal(jax.random.fold_in(key, 12), (N1, W), jnp.float32)
    marked = jnp.any(jnp.arange(N1, dtype=jnp.int32)[:, None] == rows_taken[None, :], axis=1)
    scales = jnp.where(marked, 0.1875, 20.0)
    return (values * scales[:, None]).astype(jnp.bfloat16)


def draw_inverse_blocks(key, part):
    factors = jax.random.normal(jax.random.fold_in(key, 21), (GROUPS, E, E), jnp.float32) / jnp.sqrt(E * 1.0)
    spread = jnp.einsum('gij,gkj->gik', factors, factors) + 0.5 * jnp.eye(E, dtype=jnp.float32)[None, :, :]
    return spread.astype(jnp.bfloat16)


def shard_levels(rng, dims, shards, smallest, largest):
    gain, own = 1.0, jax.random.fold_in(rng, 6)
    for dim, shards_of in shards:
        draws = jnp.exp(jax.random.uniform(jax.random.fold_in(own, dim), (shards_of,), jnp.float32, smallest / len(shards), largest / len(shards)))
        gain = gain * jnp.repeat(draws, dims[dim] // shards_of).reshape([-1 if axis == dim else 1 for axis in range(len(dims))])
    return gain


def noise(key, shape, deviation, limit, cuts=(), kind=jnp.bfloat16):
    entries = deviation * jax.random.normal(key, shape, jnp.float32)
    if cuts:
        entries = entries * shard_levels(key, shape, cuts, -0.22, 0.18)
    return jnp.clip(entries, -limit, limit).astype(kind)


def setup_inputs(seed: int = 0) -> dict:
    splits = jax.random.split(jax.random.key(seed), 7)
    return {
        "border": noise(splits[0], (GROUPS, N1, E), 0.25, 1.5, ((0, 4), (1, 8))),
        "inverse_blocks": draw_inverse_blocks(jax.random.fold_in(splits[6], 71), 0),
        "selected": draw_selected(jax.random.fold_in(splits[6], 71), 0),
        "assignment": jax.random.permutation(splits[3], GROUPS).astype(jnp.int32),
        "probability": jnp.clip(jnp.exp(jax.random.uniform(splits[4], (GROUPS,), jnp.float32, math.log(2.0), math.log(8.0))), 2.0, 8.0),
        "prior_panel": draw_prior_panel(jax.random.fold_in(splits[6], 71), 0),
    }


def reference(border, inverse_blocks, selected, assignment, probability, prior_panel):
    groups = border.shape[0]
    rank_list = jnp.arange(groups, dtype=jnp.int32)
    weights = lax.optimization_barrier(jnp.sum(jnp.where(assignment[:, None] == rank_list[None, :], probability[None, :], 0.0), axis=1))

    def add_group(schur_sum, members):
        scenario_rows, inverse, weight = members
        picked = jnp.take(scenario_rows, selected, axis=0)
        project = lax.dot_general(inverse.astype(jnp.float32), picked.astype(jnp.float32), (((1,), (1,)), ((), ())), preferred_element_type=jnp.float32).astype(jnp.bfloat16)
        return (schur_sum + weight * jnp.dot(scenario_rows.astype(jnp.float32), project.astype(jnp.float32), preferred_element_type=jnp.float32), None)
    schur_sum, unused = lax.scan(add_group, jnp.zeros((N1, W), jnp.float32), (border, inverse_blocks, weights))
    prior_sel = jnp.take(prior_panel, selected, axis=0)
    schur_panel = schur_sum - lax.dot_general(prior_panel.astype(jnp.float32), prior_sel.astype(jnp.float32), (((1,), (1,)), ((), ())), preferred_element_type=jnp.float32)
    corner = jnp.take(schur_panel, selected, axis=0)
    factor = jnp.linalg.cholesky(corner)
    solved = jax.scipy.linalg.solve_triangular(factor, schur_panel.T, lower=True).T
    marked = jnp.any(jnp.arange(N1, dtype=jnp.int32)[:, None] == selected[None, :], axis=1)
    panel_out = jnp.where(marked[:, None], 0.0, solved)
    rounded = panel_out.astype(jnp.bfloat16)

    def group_product(scenario_rows):
        return lax.dot_general(scenario_rows.astype(jnp.float32), rounded.astype(jnp.float32), (((0,), (0,)), ((), ())), preferred_element_type=jnp.float32) / math.sqrt(N1)
    residual = lax.map(group_product, border)
    return (panel_out, residual)
```

```python
import functools
import math

import jax
import jax.numpy as jnp
from jax import lax
from jax.experimental import pallas as pl
from jax.experimental.pallas import tpu as pltpu
from jax.sharding import PartitionSpec as P

N1 = 131072
LANES = 4
EXTRA = 16
TILE_BITS = 4
BLOCK = 64
PIVOTS = 4
STEP = 512
VMEM = 60 * 1024 * 1024
VMEM_SOME = 24 * 1024 * 1024
SMALL = pl.CostEstimate(flops=1 << 16, bytes_accessed=1 << 12, transcendentals=0)
F32, BF16 = jnp.float32, jnp.bfloat16


def swap(value, axis, size, bit):
    return lax.ppermute(value, axis, [(i, i ^ (1 << bit)) for i in range(size)])


def after(value, done):
    return lax.optimization_barrier((value, done))[0]


def bit_of(index, bit):
    return (index >> bit) & 1


def pick_kernel(place_ref, sel_ref, border_ref, prior_ref, keep_ref, away_ref, btile, ptile, rows, blist, plist, bsem, psem):
    count = sel_ref.shape[0]
    wide = border_ref.shape[1]
    height, own = border_ref.shape[0], prior_ref.shape[0]
    b_first, p_first, mask = place_ref[0], place_ref[1], place_ref[2]

    def scan(j, found):
        b_found, p_found = found
        b_off, p_off = sel_ref[j] - b_first, sel_ref[j] - p_first
        blist[b_found] = j
        plist[p_found] = j
        b_in = (b_off >= 0) & (b_off < height)
        p_in = (p_off >= 0) & (p_off < own)
        return b_found + b_in.astype(jnp.int32), p_found + p_in.astype(jnp.int32)

    b_found, p_found = lax.fori_loop(0, count, scan, (jnp.int32(0), jnp.int32(0)), unroll=8)

    def copy(source, first, at, tiles, sems, slot):
        base = pl.multiple_of(((at - first) >> TILE_BITS) << TILE_BITS, 1 << TILE_BITS)
        return pltpu.make_async_copy(source.at[pl.ds(base, 1 << TILE_BITS)], tiles.at[slot], sems.at[slot])

    def start(source, first, names, tiles, sems):
        def step(i, carry):
            copy(source, first, sel_ref[names[i]], tiles, sems, i).start()
            return carry

        return step

    def finish(source, first, names, tiles, sems, columns):
        def step(i, carry):
            j = names[i]
            at = sel_ref[j]
            copy(source, first, at, tiles, sems, i).wait()
            tile = tiles[i].astype(F32)
            ids = lax.broadcasted_iota(jnp.int32, tile.shape, 0)
            row = jnp.where(ids == ((at - first) & ((1 << TILE_BITS) - 1)), tile, 0.0)
            rows[pl.ds(j ^ mask, 1), columns] = jnp.sum(row, axis=0, keepdims=True)
            return carry

        return step

    b_args = (border_ref, b_first, blist, btile, bsem)
    p_args = (prior_ref, p_first, plist, ptile, psem)
    lax.fori_loop(0, b_found, start(*b_args), 0)
    lax.fori_loop(0, p_found, start(*p_args), 0)
    rows[...] = jnp.zeros_like(rows)
    lax.fori_loop(0, b_found, finish(*b_args, slice(0, wide)), 0)
    lax.fori_loop(0, p_found, finish(*p_args, slice(wide, rows.shape[1])), 0)
    keep_ref[...] = rows[: count // 2, :].astype(BF16)
    away_ref[...] = rows[count // 2 :, :].astype(BF16)


def pick_rows(my_rows, prior_panel, selected, place):
    count = selected.shape[0]
    wide, narrow = my_rows.shape[1], prior_panel.shape[1]
    return pl.pallas_call(
        pick_kernel,
        out_shape=[jax.ShapeDtypeStruct((count // 2, wide + narrow), BF16)] * 2,
        in_specs=[
            pl.BlockSpec(memory_space=pltpu.SMEM),
            pl.BlockSpec(memory_space=pltpu.SMEM),
            pl.BlockSpec(memory_space=pl.ANY),
            pl.BlockSpec(memory_space=pl.ANY),
        ],
        out_specs=[pl.BlockSpec(memory_space=pltpu.VMEM)] * 2,
        scratch_shapes=[
            pltpu.VMEM((count, 1 << TILE_BITS, wide), BF16),
            pltpu.VMEM((count, 1 << TILE_BITS, narrow), BF16),
            pltpu.VMEM((count, wide + narrow), F32),
            pltpu.SMEM((count,), jnp.int32),
            pltpu.SMEM((count,), jnp.int32),
            pltpu.SemaphoreType.DMA((count,)),
            pltpu.SemaphoreType.DMA((count,)),
        ],
        compiler_params=pltpu.CompilerParams(vmem_limit_bytes=VMEM),
        cost_estimate=SMALL,
        name="pick_rows",
    )(place, selected, my_rows, prior_panel)


def place_matrix(mask, count, dtype):
    place = lax.broadcasted_iota(jnp.int32, (count, count), 0)
    column = lax.broadcasted_iota(jnp.int32, (count, count), 1)
    return jnp.where((column ^ mask) == place, 1.0, 0.0).astype(dtype)


def project_kernel(place_ref, weight_ref, inverse_ref, half_ref, other_ref, share_ref, project_ref, payload_ref):
    count = project_ref.shape[1]
    wide = half_ref.shape[1]

    def times(rows):
        return lax.dot_general(inverse_ref[0], rows, (((1,), (1,)), ((), ())), preferred_element_type=F32).astype(BF16)

    placed = jnp.concatenate([times(half_ref[...]), times(other_ref[...])], axis=1)
    project = jnp.dot(placed, place_matrix(place_ref[2], count, BF16), preferred_element_type=F32).astype(BF16)
    project_ref[...] = project
    payload_ref[:, :count] = weight_ref[0] * jnp.dot(share_ref[:, :wide], project, preferred_element_type=F32)
    payload_ref[:, count:] = share_ref[:, wide:].astype(F32)


def make_project(place, weight, inverse_blocks, half, other, share):
    wide = inverse_blocks.shape[1]
    count = 2 * half.shape[0]
    part = share.shape[0]
    vmem = pl.BlockSpec(memory_space=pltpu.VMEM)
    smem = pl.BlockSpec(memory_space=pltpu.SMEM)
    return pl.pallas_call(
        project_kernel,
        in_specs=[smem, smem, vmem, vmem, vmem, vmem],
        out_specs=[vmem, vmem],
        out_shape=[jax.ShapeDtypeStruct((wide, count), BF16), jax.ShapeDtypeStruct((part, 2 * count), F32)],
        compiler_params=pltpu.CompilerParams(vmem_limit_bytes=VMEM_SOME),
        cost_estimate=SMALL,
        name="make_project",
    )(place, weight, inverse_blocks, half, other, share)


def chunk_copies(lane, parts, ids_ref, border_ref, held, sem, got_refs, got_held, got_sems):
    step = held.shape[1]
    blocks = held.shape[0] // parts
    copies, got_copies = [], [[] for _ in got_refs]
    for j in range(parts):
        for t in range(blocks):
            slot = j * blocks + t
            source = border_ref.at[ids_ref[j], lane, pl.ds(t * step, step)]
            copies.append(pltpu.make_async_copy(source, held.at[slot], sem.at[slot]))
            for g, got_ref in enumerate(got_refs):
                source = got_ref.at[ids_ref[parts * (g + 1) + j], t]
                got_copies[g].append(pltpu.make_async_copy(source, got_held[g].at[slot], got_sems[g].at[slot]))
    for slot in range(len(copies)):
        copies[slot].start()
        for one in got_copies:
            one[slot].start()
    return copies, list(zip(got_copies, got_held))


def send_kernel(lane, parts, gots, ids_ref, border_ref, project_ref, weight_ref, *refs):
    got_refs, out_ref = refs[:gots], refs[gots]
    scratch = refs[gots + 1 :]
    held, sem, got_held, got_sems = scratch[0], scratch[1], scratch[2 : 2 + gots], scratch[2 + gots :]
    copies, incoming = chunk_copies(lane, parts, ids_ref, border_ref, held, sem, got_refs, got_held, got_sems)
    blocks = held.shape[0] // parts
    for slot in range(len(copies)):
        copies[slot].wait()
        total = jnp.dot(held[slot], project_ref[...], preferred_element_type=F32) * weight_ref[0]
        rows, cols = total.shape
        for got_copies, got in incoming:
            got_copies[slot].wait()
            power = got[slot, rows : rows + EXTRA, :].astype(F32)[0:1, :]
            total = total + got[slot, :rows, :].astype(F32) * jnp.exp2(power)
        largest = jnp.maximum(jnp.max(jnp.abs(total), axis=0, keepdims=True), 1e-30)
        power = jnp.ceil(jnp.log2(largest)) - 15.0
        whole = jnp.clip(jnp.round(total * jnp.exp2(-power)), -32767.0, 32767.0)
        out_ref[slot // blocks, slot % blocks, :rows, :] = whole.astype(jnp.int32).astype(jnp.int16)
        out_ref[slot // blocks, slot % blocks, rows:, :] = (
            jnp.broadcast_to(power, (EXTRA, cols)).astype(jnp.int32).astype(jnp.int16)
        )


def chunk_scratch(slots, step, wide, cols, gots):
    shapes = [pltpu.VMEM((slots, step, wide), BF16), pltpu.SemaphoreType.DMA((slots,))]
    shapes += [pltpu.VMEM((slots, step + EXTRA, cols), jnp.int16)] * gots
    return shapes + [pltpu.SemaphoreType.DMA((slots,))] * gots


def send_sum(border4, lane, ids, project, weight, gots):
    _, _, rows, wide = border4.shape
    cols = project.shape[1]
    parts = ids.shape[0] // (len(gots) + 1)
    step = min(rows, STEP)
    blocks = rows // step
    vmem = pl.BlockSpec(memory_space=pltpu.VMEM)
    smem = pl.BlockSpec(memory_space=pltpu.SMEM)
    hbm = pl.BlockSpec(memory_space=pl.ANY)
    return pl.pallas_call(
        functools.partial(send_kernel, lane, parts, len(gots)),
        in_specs=[smem, hbm, vmem, smem] + [hbm] * len(gots),
        out_specs=vmem,
        out_shape=jax.ShapeDtypeStruct((parts, blocks, step + EXTRA, cols), jnp.int16),
        scratch_shapes=chunk_scratch(parts * blocks, step, wide, cols, len(gots)),
        compiler_params=pltpu.CompilerParams(vmem_limit_bytes=VMEM_SOME),
        cost_estimate=pl.CostEstimate(flops=1 << 16, bytes_accessed=12 << 20, transcendentals=0),
        name="send_sum",
    )(ids, border4, project, weight, *gots)


def factor_kernel(place_ref, half_ref, other_ref, prior_ref, high_ref, low_ref, work):
    count = 2 * half_ref.shape[0]
    exact = lax.Precision.HIGHEST
    turn = place_matrix(place_ref[2], count, F32)

    def placed(columns):
        rows = jnp.concatenate([half_ref[:, columns], other_ref[:, columns]], axis=0)
        return lax.dot_general(turn, rows, (((0,), (0,)), ((), ())), preferred_element_type=F32, precision=exact)

    prior_sel = placed(slice(count, 2 * count)).astype(BF16)
    prior_ref[...] = prior_sel
    corner = placed(slice(0, count)) - lax.dot_general(
        prior_sel, prior_sel, (((1,), (1,)), ((), ())), preferred_element_type=F32
    )
    work[:, :count] = 0.5 * (corner + corner.T)
    work[:, count:] = jnp.where(
        lax.broadcasted_iota(jnp.int32, (count, count), 0) == lax.broadcasted_iota(jnp.int32, (count, count), 1), 1.0, 0.0
    )
    side = min(count, BLOCK)
    for k in range(count // side):
        low, high = k * side, (k + 1) * side
        same = jnp.where(
            lax.broadcasted_iota(jnp.int32, (side, side), 0) == lax.broadcasted_iota(jnp.int32, (side, side), 1), 1.0, 0.0
        )
        tiles = jnp.concatenate([work[low:high, low:high], same], axis=1)
        tiles = [tiles[8 * i : 8 * i + 8, :] for i in range(side // 8)]
        row_ids = lax.broadcasted_iota(jnp.int32, tiles[0].shape, 0)
        for j in range(0, side, PIVOTS):
            home, inner = j // 8, j % 8
            lanes = tiles[0].shape[1]
            columns = [
                [jnp.broadcast_to(tile[:, j + q : j + q + 1], tile.shape) for tile in tiles[home:]] for q in range(PIVOTS)
            ]
            rows = [tiles[home][inner + q : inner + q + 1, :] for q in range(PIVOTS)]
            for q in range(PIVOTS):
                pivot = columns[q][0][inner + q : inner + q + 1, :]
                scale = lax.rsqrt(pivot)
                scale = scale * (1.5 - 0.5 * pivot * scale * scale)
                rows[q] = rows[q] * scale
                columns[q] = [column * scale for column in columns[q]]
                for r in range(q + 1, PIVOTS):
                    entry = columns[q][0][inner + r : inner + r + 1, :]
                    rows[r] = rows[r] - entry * rows[q]
                    columns[r] = [a - entry * b for a, b in zip(columns[r], columns[q])]
            for i in range(home, side // 8):
                new = tiles[i]
                for q in range(PIVOTS):
                    new = new - columns[q][i - home] * rows[q]
                if i == home:
                    new = jnp.where(row_ids >= inner + PIVOTS, new, tiles[i])
                    for q in range(PIVOTS):
                        new = jnp.where(row_ids == inner + q, rows[q], new)
                tiles[i] = new
        inverse = jnp.concatenate([tile[:, side:] for tile in tiles], axis=0)
        block = jnp.dot(inverse, work[low:high, :], preferred_element_type=F32, precision=exact)
        work[low:high, :] = block
        if high < count:
            work[high:, :] = work[high:, :] - lax.dot_general(
                block[:, high:count], block, (((0,), (0,)), ((), ())), preferred_element_type=F32, precision=exact
            )
    inverse = work[:, count:]
    top = inverse.astype(BF16)
    high_ref[...] = top
    low_ref[...] = (inverse - top.astype(F32)).astype(BF16)


def factor_inverse(place, half, other):
    count = 2 * half.shape[0]
    vmem = pl.BlockSpec(memory_space=pltpu.VMEM)
    return pl.pallas_call(
        factor_kernel,
        in_specs=[pl.BlockSpec(memory_space=pltpu.SMEM), vmem, vmem],
        out_specs=[vmem, vmem, vmem],
        out_shape=[jax.ShapeDtypeStruct((count, count), BF16)] * 3,
        scratch_shapes=[pltpu.VMEM((count, 2 * count), F32)],
        compiler_params=pltpu.CompilerParams(vmem_limit_bytes=VMEM),
        cost_estimate=SMALL,
        name="factor_inverse",
    )(place, half, other)


def panel_kernel(lane, gots, aliased, ids_ref, border_ref, project_ref, weight_ref, *refs):
    got_refs, refs = refs[:gots], refs[gots:]
    first_ref, prior_ref, prior_sel_ref, high_ref, low_ref, sel_ref = refs[:6]
    out_ref, turned_ref = refs[6 + aliased : 8 + aliased]
    scratch = refs[8 + aliased :]
    held, sem, got_held, got_sems = scratch[0], scratch[1], scratch[2 : 2 + gots], scratch[2 + gots :]
    copies, incoming = chunk_copies(lane, 1, ids_ref, border_ref, held, sem, got_refs, got_held, got_sems)

    def times(a, b):
        return lax.dot_general(a, b, (((1,), (1,)), ((), ())), preferred_element_type=F32)

    for slot in range(len(copies)):
        rows = held.shape[1]
        here = slice(slot * rows, (slot + 1) * rows)
        copies[slot].wait()
        total = jnp.dot(held[slot], project_ref[...], preferred_element_type=F32) * weight_ref[0]
        total = total - times(prior_ref[here, :], prior_sel_ref[...])
        for got_copies, got in incoming:
            got_copies[slot].wait()
            power = got[slot, rows : rows + EXTRA, :].astype(F32)[0:1, :]
            total = total + got[slot, :rows, :].astype(F32) * jnp.exp2(power)
        high = total.astype(BF16)
        low = (total - high.astype(F32)).astype(BF16)
        solved = times(high, high_ref[...]) + (times(low, high_ref[...]) + times(high, low_ref[...]))
        ids = first_ref[0] + slot * rows + lax.broadcasted_iota(jnp.int32, (rows, 1), 0)
        hits = jnp.where(ids == sel_ref[0:1, :], 1.0, 0.0)
        marked = jnp.max(hits, axis=1, keepdims=True)
        solved = jnp.where(marked > 0.0, 0.0, solved)
        out_ref[here, :] = solved
        turned_ref[:, here] = jnp.transpose(solved.astype(BF16))


def panel_rows(border4, lane, ids, project, weight, gots, first, prior_panel, prior_sel, high, low, sel8, done):
    _, lanes, rows, wide = border4.shape
    own, cols = prior_panel.shape
    step = min(rows, STEP)
    vmem = pl.BlockSpec(memory_space=pltpu.VMEM)
    smem = pl.BlockSpec(memory_space=pltpu.SMEM)
    hbm = pl.BlockSpec(memory_space=pl.ANY)
    mine = pl.BlockSpec((rows, cols), lambda t: (lane, 0))
    in_specs = [smem, hbm, vmem, smem] + [hbm] * len(gots) + [smem, mine, vmem, vmem, vmem, vmem]
    args = [ids, border4, project, weight, *gots, first, prior_panel, prior_sel, high, low, sel8]
    aliases = {}
    if done is not None:
        in_specs.append(hbm)
        args.append(done)
        aliases = {len(args) - 1: 0}
    return pl.pallas_call(
        functools.partial(panel_kernel, lane, len(gots), len(aliases)),
        grid=(1,),
        in_specs=in_specs,
        out_specs=[mine, vmem],
        out_shape=[jax.ShapeDtypeStruct((own, cols), F32), jax.ShapeDtypeStruct((cols, rows), BF16)],
        input_output_aliases=aliases,
        scratch_shapes=chunk_scratch(rows // step, step, wide, cols, len(gots)),
        compiler_params=pltpu.CompilerParams(vmem_limit_bytes=VMEM_SOME),
        cost_estimate=pl.CostEstimate(flops=1 << 16, bytes_accessed=16 << 20, transcendentals=0),
        name="panel_rows",
    )(*args)


def residual_kernel(lane, parts, ids_ref, border_ref, *refs):
    turned, out_ref, held, sems = refs[:parts], refs[-3], refs[-2], refs[-1]
    before = refs[parts] if len(refs) > parts + 3 else None
    rows = turned[0].shape[1]
    step = held.shape[1]
    blocks = rows // step
    copies = []
    for j in range(parts):
        for t in range(blocks):
            slot = j * blocks + t
            source = border_ref.at[ids_ref[j], lane, pl.ds(t * step, step)]
            copies.append(pltpu.make_async_copy(source, held.at[slot], sems.at[slot]))
    for copy in copies:
        copy.start()
    for slot, copy in enumerate(copies):
        copy.wait()
        j, t = slot // blocks, slot % blocks
        product = jnp.dot(turned[j][:, t * step : (t + 1) * step], held[slot], preferred_element_type=F32)
        if slot == 0:
            out_ref[...] = product if before is None else before[...] + product
        else:
            out_ref[...] += product


def residual_add(border4, lane, pieces, total):
    _, _, rows, wide = border4.shape
    cols = pieces[0][0].shape[0]
    parts = len(pieces)
    step = min(rows, STEP)
    slots = parts * (rows // step)
    ids = jnp.stack([at for _, at in pieces]).astype(jnp.int32)
    vmem = pl.BlockSpec(memory_space=pltpu.VMEM)
    args = [ids, border4] + [block for block, _ in pieces]
    aliases = {}
    if total is not None:
        args.append(total)
        aliases = {len(args) - 1: 0}
    return pl.pallas_call(
        functools.partial(residual_kernel, lane, parts),
        in_specs=[pl.BlockSpec(memory_space=pltpu.SMEM), pl.BlockSpec(memory_space=pl.ANY)] + [vmem] * (len(args) - 2),
        out_specs=vmem,
        out_shape=jax.ShapeDtypeStruct((cols, wide), F32),
        input_output_aliases=aliases,
        scratch_shapes=[pltpu.VMEM((slots, step, wide), BF16), pltpu.SemaphoreType.DMA((slots,))],
        compiler_params=pltpu.CompilerParams(vmem_limit_bytes=VMEM_SOME),
        cost_estimate=pl.CostEstimate(flops=1 << 16, bytes_accessed=12 << 20, transcendentals=0),
        name="residual_add",
    )(*args)


def body(border, inverse_blocks, selected, assignment, probability, prior_panel):
    groups = lax.axis_size("grp")
    members = lax.axis_size("dev")
    group_index = lax.axis_index("grp")
    member = lax.axis_index("dev")
    group_bits = groups.bit_length() - 1
    member_bits = members.bit_length() - 1
    my_rows = border[0]
    height, wide = my_rows.shape
    own_rows, cols = prior_panel.shape
    lanes = min(LANES, own_rows // 128)
    lane_rows = own_rows // lanes
    border4 = my_rows.reshape(groups, lanes, lane_rows, wide)
    first_row = (member * groups + group_index) * own_rows

    rank_list = jnp.arange(groups, dtype=jnp.int32)
    scenario = jnp.sum(jnp.where(rank_list == group_index, assignment, 0))
    weight = jnp.sum(jnp.where(rank_list == scenario, probability, 0.0))

    chips = members // 2
    part = selected.shape[0] // members
    mask = bit_of(member, 0) * (selected.shape[0] // 2) + (member >> 1) * part
    place = jnp.stack([member * height, first_row, mask]).astype(jnp.int32)

    def to_chip(block, shift):
        return lax.ppermute(block, "dev", [(i, i ^ (shift << 1)) for i in range(members)])

    def gather_members(block):
        half = jnp.concatenate([block] + [to_chip(block, shift) for shift in range(1, chips)], axis=0)
        return half, swap(half, "dev", members, 0)

    keep, away = pick_rows(my_rows, prior_panel, selected, place)
    held = keep + swap(away, "dev", members, 0)
    got = [to_chip(held[shift * part : (shift + 1) * part], shift) for shift in range(1, chips)]
    share = functools.reduce(jnp.add, got, held[:part])
    half, other = gather_members(share[:, :wide])
    weight = weight.reshape(1)
    project, summed = make_project(place, weight, inverse_blocks, half, other, share)
    sel8 = jnp.broadcast_to(selected[None, :], (8, selected.shape[0]))

    def orders(lane):
        shift = lane % group_bits
        return [(shift + i) % group_bits for i in range(group_bits)]

    def listing(order, done, flip):
        fixed = group_index ^ (flip << order[done]) if flip else group_index
        settled = done + 1 if flip else done
        free = order[settled:]
        found = []
        for j in range(1 << len(free)):
            value = fixed
            for i, bit in enumerate(free):
                value = (value & ~(1 << bit)) | (((j >> (len(free) - 1 - i)) & 1) << bit)
            found.append(value)
        return found

    def place_in(order, settled, quarter):
        index = 0
        for bit in order[settled:]:
            index = 2 * index + bit_of(quarter, bit)
        return index

    def stage_ids(order, stage):
        quarters = listing(order, stage, 1) if stage < group_bits else [group_index]
        ids = list(quarters)
        for earlier in range(stage):
            ids += [place_in(order, earlier + 1, quarter) for quarter in quarters]
        return jnp.stack([jnp.asarray(at, jnp.int32) for at in ids])

    gots = [[] for _ in range(lanes)]

    def send_stage(lane, stage, token, held_back=None):
        order = orders(lane)
        ids = after(stage_ids(order, stage), token)
        sent = send_sum(border4, lane, ids, project, weight, gots[lane])
        if held_back is not None:
            sent = after(sent, held_back)
        gots[lane].append(swap(sent, "grp", groups, order[stage]))
        return sent

    token = project
    for lane in range(lanes):
        if lane < group_bits:
            summed = summed + swap(summed, "grp", groups, lane)
            token = send_stage(lane, 0, token, summed)
        else:
            token = send_stage(lane, 0, token)
    for bit in range(lanes, group_bits):
        summed = summed + swap(summed, "grp", groups, bit)
    corner_half, corner_other = gather_members(summed)
    early = lanes // 2
    for stage in range(1, group_bits):
        for lane in range(early):
            token = send_stage(lane, stage, token)
    prior_sel, inverse_high, inverse_low = factor_inverse(place, corner_half, after(corner_other, token))
    token = prior_sel
    for stage in range(1, group_bits):
        for lane in range(early, lanes):
            token = send_stage(lane, stage, token)

    panel_out, total = None, None
    pieces, first_more = [], []
    for lane in range(lanes):
        order = orders(lane)
        first = (first_row + lane * lane_rows).reshape(1).astype(jnp.int32)
        ids = after(stage_ids(order, group_bits), token)
        panel_out, turned = panel_rows(
            border4, lane, ids, project, weight, gots[lane], first,
            prior_panel, prior_sel, inverse_high, inverse_low, sel8, panel_out,
        )
        token = turned
        own = [(turned, group_index)]
        pieces.append(own)
        first_more.append([(swap(block, "grp", groups, order[0]), at ^ (1 << order[0])) for block, at in own])
    last_more = []
    for lane in range(lanes):
        order = orders(lane)
        more = [(after(block, token), at) for block, at in first_more[lane]]
        now = pieces[lane] + more
        for bit in order[1:]:
            more = [(swap(block, "grp", groups, bit), at ^ (1 << bit)) for block, at in now]
            if bit == order[-1]:
                total = residual_add(border4, lane, now, total)
                token = total
                last_more.append(more)
            now = now + more
    for lane in range(lanes):
        total = residual_add(border4, lane, last_more[lane], total)

    block = wide // members
    held = total.reshape((cols,) + (2,) * member_bits + (block,))
    for bit in range(member_bits):
        mine = bit_of(member, bit)
        axis = held.ndim - 2
        away = lax.dynamic_index_in_dim(held, 1 - mine, axis, keepdims=False)
        held = lax.dynamic_index_in_dim(held, mine, axis, keepdims=False) + swap(away, "dev", members, bit)
    residual = held.T / math.sqrt(N1)
    return (panel_out, residual[None])


def solution(mesh):
    return jax.shard_map(
        body,
        mesh=mesh,
        in_specs=(
            P("grp", "dev", None),
            P("grp", None, None),
            P(),
            P(),
            P(),
            P(("dev", "grp"), None),
        ),
        out_specs=(P(("dev", "grp"), None), P("grp", "dev", None)),
        check_vma=False,
    )
```

```python
import functools
import math

import jax
import jax.numpy as jnp
from jax import lax
from jax.experimental import pallas as pl
from jax.experimental.pallas import tpu as pltpu
from jax.sharding import PartitionSpec as P

N1 = 131072
LANES = 4
EXTRA = 16
TILE_BITS = 4
PIVOTS = 4
STEP = 512
EXACT = lax.Precision.HIGHEST
VMEM = 60 * 1024 * 1024
VMEM_SOME = 32 * 1024 * 1024
SMALL = pl.CostEstimate(flops=1 << 16, bytes_accessed=1 << 12, transcendentals=0)
F32, BF16 = jnp.float32, jnp.bfloat16


def swap(value, axis, size, bit):
    return lax.ppermute(value, axis, [(i, i ^ (1 << bit)) for i in range(size)])


def after(value, done):
    return lax.optimization_barrier((value, done))[0]


def bit_of(index, bit):
    return (index >> bit) & 1


def pick_kernel(place_ref, sel_ref, border_ref, prior_ref, keep_ref, away_ref, btile, ptile, rows, names, bsem, psem):
    count = sel_ref.shape[0]
    wide = border_ref.shape[1]
    height, own = border_ref.shape[0], prior_ref.shape[0]
    b_first, p_first, mask = place_ref[0], place_ref[1], place_ref[2]
    tile_rows = 1 << TILE_BITS

    def scan(j, found):
        offset = sel_ref[j] - b_first
        names[found] = j
        return found + ((offset >= 0) & (offset < height)).astype(jnp.int32)

    found = lax.fori_loop(0, count, scan, jnp.int32(0), unroll=16)

    def copies(i):
        at = sel_ref[names[i]]
        b_off, p_off = at - b_first, at - p_first
        p_in = (p_off >= 0) & (p_off < own)
        p_off = jnp.clip(p_off, 0, own - 1)
        b_base = pl.multiple_of((b_off >> TILE_BITS) << TILE_BITS, tile_rows)
        p_base = pl.multiple_of((p_off >> TILE_BITS) << TILE_BITS, tile_rows)
        b_copy = pltpu.make_async_copy(border_ref.at[pl.ds(b_base, tile_rows)], btile.at[i], bsem.at[i])
        p_copy = pltpu.make_async_copy(prior_ref.at[pl.ds(p_base, tile_rows)], ptile.at[i], psem.at[i])
        return b_copy, p_copy, p_in, b_off - b_base, p_off - p_base

    def start(i, carry):
        b_copy, p_copy, p_in, _, _ = copies(i)
        b_copy.start()
        pl.when(p_in)(p_copy.start)
        return carry

    def wait(i, carry):
        b_copy, p_copy, p_in, _, _ = copies(i)
        b_copy.wait()
        pl.when(p_in)(p_copy.wait)
        return carry

    def place_four(q, carry):
        for u in range(4):
            i = jnp.minimum(4 * q + u, found - 1)
            _, _, p_in, b_row, p_row = copies(i)
            at = names[i] ^ mask
            ids = lax.broadcasted_iota(jnp.int32, btile.shape[1:], 0)
            row = jnp.where(ids == b_row, btile[i].astype(F32), 0.0)
            rows[pl.ds(at, 1), :wide] = jnp.sum(row, axis=0, keepdims=True)
            ids = lax.broadcasted_iota(jnp.int32, ptile.shape[1:], 0)
            row = jnp.where((ids == p_row) & p_in, ptile[i].astype(F32), 0.0)
            rows[pl.ds(at, 1), wide:] = jnp.sum(row, axis=0, keepdims=True)
        return carry

    lax.fori_loop(0, found, start, 0)
    rows[...] = jnp.zeros_like(rows)
    lax.fori_loop(0, found, wait, 0)
    lax.fori_loop(0, (found + 3) >> 2, place_four, 0)
    keep_ref[...] = rows[: count // 2, :].astype(BF16)
    away_ref[...] = rows[count // 2 :, :].astype(BF16)


def pick_rows(my_rows, prior_panel, selected, place):
    count = selected.shape[0]
    wide, narrow = my_rows.shape[1], prior_panel.shape[1]
    return pl.pallas_call(
        pick_kernel,
        out_shape=[jax.ShapeDtypeStruct((count // 2, wide + narrow), BF16)] * 2,
        in_specs=[
            pl.BlockSpec(memory_space=pltpu.SMEM),
            pl.BlockSpec(memory_space=pltpu.SMEM),
            pl.BlockSpec(memory_space=pl.ANY),
            pl.BlockSpec(memory_space=pl.ANY),
        ],
        out_specs=[pl.BlockSpec(memory_space=pltpu.VMEM)] * 2,
        scratch_shapes=[
            pltpu.VMEM((count, 1 << TILE_BITS, wide), BF16),
            pltpu.VMEM((count, 1 << TILE_BITS, narrow), BF16),
            pltpu.VMEM((count, wide + narrow), F32),
            pltpu.SMEM((count,), jnp.int32),
            pltpu.SemaphoreType.DMA((count,)),
            pltpu.SemaphoreType.DMA((count,)),
        ],
        compiler_params=pltpu.CompilerParams(vmem_limit_bytes=VMEM),
        cost_estimate=SMALL,
        name="pick_rows",
    )(place, selected, my_rows, prior_panel)


def place_matrix(mask, count, dtype):
    place = lax.broadcasted_iota(jnp.int32, (count, count), 0)
    column = lax.broadcasted_iota(jnp.int32, (count, count), 1)
    return jnp.where((column ^ mask) == place, 1.0, 0.0).astype(dtype)


def project_kernel(place_ref, weight_ref, inverse_ref, half_ref, other_ref, share_ref, project_ref, payload_ref):
    count = project_ref.shape[1]
    wide = half_ref.shape[1]

    def times(rows):
        return lax.dot_general(inverse_ref[0], rows, (((1,), (1,)), ((), ())), preferred_element_type=F32).astype(BF16)

    placed = jnp.concatenate([times(half_ref[...]), times(other_ref[...])], axis=1)
    project = jnp.dot(placed, place_matrix(place_ref[2], count, BF16), preferred_element_type=F32).astype(BF16)
    project_ref[...] = project
    payload_ref[:, :count] = weight_ref[0] * jnp.dot(share_ref[:, :wide], project, preferred_element_type=F32)
    payload_ref[:, count:] = share_ref[:, wide:].astype(F32)


def make_project(place, weight, inverse_blocks, half, other, share):
    wide = inverse_blocks.shape[1]
    count = 2 * half.shape[0]
    part = share.shape[0]
    vmem = pl.BlockSpec(memory_space=pltpu.VMEM)
    smem = pl.BlockSpec(memory_space=pltpu.SMEM)
    return pl.pallas_call(
        project_kernel,
        in_specs=[smem, smem, vmem, vmem, vmem, vmem],
        out_specs=[vmem, vmem],
        out_shape=[jax.ShapeDtypeStruct((wide, count), BF16), jax.ShapeDtypeStruct((part, 2 * count), F32)],
        compiler_params=pltpu.CompilerParams(vmem_limit_bytes=VMEM_SOME),
        cost_estimate=SMALL,
        name="make_project",
    )(place, weight, inverse_blocks, half, other, share)


def chunk_copies(lane, parts, ids_ref, border_ref, held, sem, got_refs, got_held, got_sems):
    step = held.shape[1]
    blocks = held.shape[0] // parts
    copies, got_copies = [], [[] for _ in got_refs]
    for j in range(parts):
        for t in range(blocks):
            slot = j * blocks + t
            source = border_ref.at[ids_ref[j], lane, pl.ds(t * step, step)]
            copies.append(pltpu.make_async_copy(source, held.at[slot], sem.at[slot]))
            for g, got_ref in enumerate(got_refs):
                source = got_ref.at[ids_ref[parts * (g + 1) + j], t]
                got_copies[g].append(pltpu.make_async_copy(source, got_held[g].at[slot], got_sems[g].at[slot]))
    for slot in range(len(copies)):
        copies[slot].start()
        for one in got_copies:
            one[slot].start()
    return copies, list(zip(got_copies, got_held))


def send_kernel(lane, parts, gots, ids_ref, border_ref, project_ref, weight_ref, *refs):
    got_refs, out_ref = refs[:gots], refs[gots]
    scratch = refs[gots + 1 :]
    held, sem, got_held, got_sems = scratch[0], scratch[1], scratch[2 : 2 + gots], scratch[2 + gots :]
    copies, incoming = chunk_copies(lane, parts, ids_ref, border_ref, held, sem, got_refs, got_held, got_sems)
    blocks = held.shape[0] // parts
    for slot in range(len(copies)):
        copies[slot].wait()
        total = jnp.dot(held[slot], project_ref[...], preferred_element_type=F32) * weight_ref[0]
        rows, cols = total.shape
        for got_copies, got in incoming:
            got_copies[slot].wait()
            power = got[slot, rows : rows + EXTRA, :].astype(F32)[0:1, :]
            total = total + got[slot, :rows, :].astype(F32) * jnp.exp2(power)
        largest = jnp.maximum(jnp.max(jnp.abs(total), axis=0, keepdims=True), 1e-30)
        power = jnp.ceil(jnp.log2(largest)) - 15.0
        whole = jnp.clip(jnp.round(total * jnp.exp2(-power)), -32767.0, 32767.0)
        out_ref[slot // blocks, slot % blocks, :rows, :] = whole.astype(jnp.int32).astype(jnp.int16)
        out_ref[slot // blocks, slot % blocks, rows:, :] = (
            jnp.broadcast_to(power, (EXTRA, cols)).astype(jnp.int32).astype(jnp.int16)
        )


def chunk_scratch(slots, step, wide, cols, gots):
    shapes = [pltpu.VMEM((slots, step, wide), BF16), pltpu.SemaphoreType.DMA((slots,))]
    shapes += [pltpu.VMEM((slots, step + EXTRA, cols), jnp.int16)] * gots
    return shapes + [pltpu.SemaphoreType.DMA((slots,))] * gots


def send_sum(border4, lane, ids, project, weight, gots):
    _, _, rows, wide = border4.shape
    cols = project.shape[1]
    parts = ids.shape[0] // (len(gots) + 1)
    step = min(rows, STEP)
    blocks = rows // step
    vmem = pl.BlockSpec(memory_space=pltpu.VMEM)
    smem = pl.BlockSpec(memory_space=pltpu.SMEM)
    hbm = pl.BlockSpec(memory_space=pl.ANY)
    return pl.pallas_call(
        functools.partial(send_kernel, lane, parts, len(gots)),
        in_specs=[smem, hbm, vmem, smem] + [hbm] * len(gots),
        out_specs=vmem,
        out_shape=jax.ShapeDtypeStruct((parts, blocks, step + EXTRA, cols), jnp.int16),
        scratch_shapes=chunk_scratch(parts * blocks, step, wide, cols, len(gots)),
        compiler_params=pltpu.CompilerParams(vmem_limit_bytes=VMEM_SOME),
        cost_estimate=pl.CostEstimate(flops=1 << 16, bytes_accessed=12 << 20, transcendentals=0),
        name="send_sum",
    )(ids, border4, project, weight, *gots)


def factor_start(place_ref, half_ref, other_ref, work_ref, prior_ref):
    count = 2 * half_ref.shape[0]
    turn = place_matrix(place_ref[2], count, F32)

    def placed(columns):
        rows = jnp.concatenate([half_ref[:, columns], other_ref[:, columns]], axis=0)
        return lax.dot_general(turn, rows, (((0,), (0,)), ((), ())), preferred_element_type=F32, precision=EXACT)

    prior_sel = placed(slice(count, 2 * count)).astype(BF16)
    prior_ref[...] = prior_sel
    corner = placed(slice(0, count)) - lax.dot_general(
        prior_sel, prior_sel, (((1,), (1,)), ((), ())), preferred_element_type=F32
    )
    work_ref[:, :count] = 0.5 * (corner + corner.T)
    work_ref[:, count:] = jnp.where(
        lax.broadcasted_iota(jnp.int32, (count, count), 0) == lax.broadcasted_iota(jnp.int32, (count, count), 1), 1.0, 0.0
    )
    factor_blocks(work_ref, 0, 2)


def factor_finish(before_ref, high_ref, low_ref, work):
    count = before_ref.shape[0]
    work[...] = before_ref[...]
    factor_blocks(work, 2, 4)
    inverse = work[:, count:]
    top = inverse.astype(BF16)
    high_ref[...] = top
    low_ref[...] = (inverse - top.astype(F32)).astype(BF16)


def factor_blocks(work, begin, end):
    count = work.shape[0]
    side = count // 4
    for k in range(begin, end):
        low, high = k * side, (k + 1) * side
        same = jnp.where(
            lax.broadcasted_iota(jnp.int32, (side, side), 0) == lax.broadcasted_iota(jnp.int32, (side, side), 1), 1.0, 0.0
        )
        tiles = jnp.concatenate([work[low:high, low:high], same], axis=1)
        tiles = [tiles[8 * i : 8 * i + 8, :] for i in range(side // 8)]
        row_ids = lax.broadcasted_iota(jnp.int32, tiles[0].shape, 0)
        for j in range(0, side, PIVOTS):
            home, inner = j // 8, j % 8
            lanes = tiles[0].shape[1]
            columns = [
                [jnp.broadcast_to(tile[:, j + q : j + q + 1], tile.shape) for tile in tiles[home:]] for q in range(PIVOTS)
            ]
            rows = [tiles[home][inner + q : inner + q + 1, :] for q in range(PIVOTS)]
            for q in range(PIVOTS):
                pivot = columns[q][0][inner + q : inner + q + 1, :]
                scale = lax.rsqrt(pivot)
                scale = scale * (1.5 - 0.5 * pivot * scale * scale)
                rows[q] = rows[q] * scale
                columns[q] = [column * scale for column in columns[q]]
                for r in range(q + 1, PIVOTS):
                    entry = columns[q][0][inner + r : inner + r + 1, :]
                    rows[r] = rows[r] - entry * rows[q]
                    columns[r] = [a - entry * b for a, b in zip(columns[r], columns[q])]
            for i in range(home, side // 8):
                new = tiles[i]
                for q in range(PIVOTS):
                    new = new - columns[q][i - home] * rows[q]
                if i == home:
                    new = jnp.where(row_ids >= inner + PIVOTS, new, tiles[i])
                    for q in range(PIVOTS):
                        new = jnp.where(row_ids == inner + q, rows[q], new)
                tiles[i] = new
        inverse = jnp.concatenate([tile[:, side:] for tile in tiles], axis=0)
        block = jnp.dot(inverse, work[low:high, :], preferred_element_type=F32, precision=EXACT)
        work[low:high, :] = block
        if high < count:
            work[high:, :] = work[high:, :] - lax.dot_general(
                block[:, high:count], block, (((0,), (0,)), ((), ())), preferred_element_type=F32, precision=EXACT
            )

def factor_call(kernel, shapes, args, scratch=()):
    vmem = pl.BlockSpec(memory_space=pltpu.VMEM)
    smem = pl.BlockSpec(memory_space=pltpu.SMEM)
    return pl.pallas_call(
        kernel,
        in_specs=[smem if arg.ndim == 1 else vmem for arg in args],
        out_specs=[vmem] * len(shapes),
        out_shape=shapes,
        scratch_shapes=list(scratch),
        compiler_params=pltpu.CompilerParams(vmem_limit_bytes=VMEM_SOME),
        cost_estimate=SMALL,
        name=kernel.__name__,
    )(*args)


def start_factor(place, half, other):
    count = 2 * half.shape[0]
    shapes = [jax.ShapeDtypeStruct((count, 2 * count), F32), jax.ShapeDtypeStruct((count, count), BF16)]
    return factor_call(factor_start, shapes, [place, half, other])


def finish_factor(work):
    count = work.shape[0]
    shapes = [jax.ShapeDtypeStruct((count, count), BF16)] * 2
    return factor_call(factor_finish, shapes, [work], [pltpu.VMEM(work.shape, F32)])


def panel_kernel(lane, gots, aliased, ids_ref, border_ref, project_ref, weight_ref, *refs):
    got_refs, refs = refs[:gots], refs[gots:]
    first_ref, prior_ref, prior_sel_ref, high_ref, low_ref, sel_ref = refs[:6]
    out_ref, turned_ref = refs[6 + aliased : 8 + aliased]
    scratch = refs[8 + aliased :]
    held, sem, got_held, got_sems = scratch[0], scratch[1], scratch[2 : 2 + gots], scratch[2 + gots :]
    copies, incoming = chunk_copies(lane, 1, ids_ref, border_ref, held, sem, got_refs, got_held, got_sems)

    def times(a, b):
        return lax.dot_general(a, b, (((1,), (1,)), ((), ())), preferred_element_type=F32)

    for slot in range(len(copies)):
        rows = held.shape[1]
        here = slice(slot * rows, (slot + 1) * rows)
        copies[slot].wait()
        total = jnp.dot(held[slot], project_ref[...], preferred_element_type=F32) * weight_ref[0]
        total = total - times(prior_ref[here, :], prior_sel_ref[...])
        for got_copies, got in incoming:
            got_copies[slot].wait()
            power = got[slot, rows : rows + EXTRA, :].astype(F32)[0:1, :]
            total = total + got[slot, :rows, :].astype(F32) * jnp.exp2(power)
        high = total.astype(BF16)
        low = (total - high.astype(F32)).astype(BF16)
        solved = times(high, high_ref[...]) + (times(low, high_ref[...]) + times(high, low_ref[...]))
        ids = first_ref[0] + slot * rows + lax.broadcasted_iota(jnp.int32, (rows, 1), 0)
        hits = jnp.where(ids == sel_ref[0:1, :], 1.0, 0.0)
        marked = jnp.max(hits, axis=1, keepdims=True)
        solved = jnp.where(marked > 0.0, 0.0, solved)
        out_ref[here, :] = solved
        turned_ref[:, here] = jnp.transpose(solved.astype(BF16))


def panel_rows(border4, lane, ids, project, weight, gots, first, prior_panel, prior_sel, high, low, sel8, done):
    _, lanes, rows, wide = border4.shape
    own, cols = prior_panel.shape
    step = min(rows, STEP)
    vmem = pl.BlockSpec(memory_space=pltpu.VMEM)
    smem = pl.BlockSpec(memory_space=pltpu.SMEM)
    hbm = pl.BlockSpec(memory_space=pl.ANY)
    mine = pl.BlockSpec((rows, cols), lambda t: (lane, 0))
    in_specs = [smem, hbm, vmem, smem] + [hbm] * len(gots) + [smem, mine, vmem, vmem, vmem, vmem]
    args = [ids, border4, project, weight, *gots, first, prior_panel, prior_sel, high, low, sel8]
    aliases = {}
    if done is not None:
        in_specs.append(hbm)
        args.append(done)
        aliases = {len(args) - 1: 0}
    return pl.pallas_call(
        functools.partial(panel_kernel, lane, len(gots), len(aliases)),
        grid=(1,),
        in_specs=in_specs,
        out_specs=[mine, vmem],
        out_shape=[jax.ShapeDtypeStruct((own, cols), F32), jax.ShapeDtypeStruct((cols, rows), BF16)],
        input_output_aliases=aliases,
        scratch_shapes=chunk_scratch(rows // step, step, wide, cols, len(gots)),
        compiler_params=pltpu.CompilerParams(vmem_limit_bytes=VMEM_SOME),
        cost_estimate=pl.CostEstimate(flops=1 << 16, bytes_accessed=16 << 20, transcendentals=0),
        name="panel_rows",
    )(*args)


def residual_kernel(lanes, ids_ref, border_ref, *refs):
    parts = len(lanes)
    pieces, out_ref, held, sems, turned, turned_sems = refs[:parts], *refs[-5:]
    before = refs[parts] if len(refs) > parts + 5 else None
    members, _, block = out_ref.shape
    step = held.shape[1]
    blocks = turned.shape[2] // step
    copies, turned_copies = [], []
    for j in range(parts):
        turned_copies.append(pltpu.make_async_copy(pieces[j], turned.at[j], turned_sems.at[j]))
        turned_copies[j].start()
        for t in range(blocks):
            slot = j * blocks + t
            source = border_ref.at[ids_ref[j], lanes[j], pl.ds(t * step, step)]
            copies.append(pltpu.make_async_copy(source, held.at[slot], sems.at[slot]))
            copies[slot].start()
    for slot, copy in enumerate(copies):
        j, t = slot // blocks, slot % blocks
        if t == 0:
            turned_copies[j].wait()
        copy.wait()
        product = jnp.dot(turned[j][:, t * step : (t + 1) * step], held[slot], preferred_element_type=F32)
        for m in range(members):
            here = product[:, m * block : (m + 1) * block]
            if slot > 0:
                out_ref[m] += here
            else:
                out_ref[m] = here if before is None else before[m] + here


def residual_add(border4, members, pieces, total):
    _, _, rows, wide = border4.shape
    cols = pieces[0][0].shape[0]
    parts = len(pieces)
    step = min(rows, STEP)
    slots = parts * (rows // step)
    ids = jnp.stack([at for _, at, _ in pieces]).astype(jnp.int32)
    vmem = pl.BlockSpec(memory_space=pltpu.VMEM)
    args = [ids, border4] + [block for block, _, _ in pieces]
    aliases = {}
    if total is not None:
        args.append(total)
        aliases = {len(args) - 1: 0}
    return pl.pallas_call(
        functools.partial(residual_kernel, [lane for _, _, lane in pieces]),
        in_specs=[pl.BlockSpec(memory_space=pltpu.SMEM)]
        + [pl.BlockSpec(memory_space=pl.ANY)] * (1 + parts)
        + [vmem] * (len(args) - 2 - parts),
        out_specs=vmem,
        out_shape=jax.ShapeDtypeStruct((members, cols, wide // members), F32),
        input_output_aliases=aliases,
        scratch_shapes=[
            pltpu.VMEM((slots, step, wide), BF16),
            pltpu.SemaphoreType.DMA((slots,)),
            pltpu.VMEM((parts, cols, rows), BF16),
            pltpu.SemaphoreType.DMA((parts,)),
        ],
        compiler_params=pltpu.CompilerParams(vmem_limit_bytes=VMEM_SOME),
        cost_estimate=pl.CostEstimate(flops=1 << 16, bytes_accessed=12 << 20, transcendentals=0),
        name="residual_add",
    )(*args)


def code_kernel(kept_ref, got_ref, sum_ref, coded_ref):
    rows, cols = kept_ref.shape[1:]
    for chip in range(kept_ref.shape[0]):
        total = kept_ref[chip] + got_ref[chip]
        sum_ref[chip] = total
        largest = jnp.maximum(jnp.max(jnp.abs(total), axis=0, keepdims=True), 1e-30)
        power = jnp.ceil(jnp.log2(largest)) - 15.0
        whole = jnp.clip(jnp.round(total * jnp.exp2(-power)), -32767.0, 32767.0)
        coded_ref[chip, :rows, :] = whole.astype(jnp.int32).astype(jnp.int16)
        coded_ref[chip, rows:, :] = jnp.broadcast_to(power, (EXTRA, cols)).astype(jnp.int32).astype(jnp.int16)


def code_sum(kept, got):
    chips, rows, cols = kept.shape
    vmem = pl.BlockSpec(memory_space=pltpu.VMEM)
    return pl.pallas_call(
        code_kernel,
        in_specs=[vmem, vmem],
        out_specs=[vmem, vmem],
        out_shape=[
            jax.ShapeDtypeStruct((chips, rows, cols), F32),
            jax.ShapeDtypeStruct((chips, rows + EXTRA, cols), jnp.int16),
        ],
        compiler_params=pltpu.CompilerParams(vmem_limit_bytes=VMEM_SOME),
        cost_estimate=SMALL,
        name="code_sum",
    )(kept, got)


def body(border, inverse_blocks, selected, assignment, probability, prior_panel):
    groups = lax.axis_size("grp")
    members = lax.axis_size("dev")
    group_index = lax.axis_index("grp")
    member = lax.axis_index("dev")
    group_bits = groups.bit_length() - 1
    member_bits = members.bit_length() - 1
    my_rows = border[0]
    height, wide = my_rows.shape
    own_rows, cols = prior_panel.shape
    lanes = min(LANES, own_rows // 128)
    lane_rows = own_rows // lanes
    border4 = my_rows.reshape(groups, lanes, lane_rows, wide)
    first_row = (member * groups + group_index) * own_rows

    rank_list = jnp.arange(groups, dtype=jnp.int32)
    scenario = jnp.sum(jnp.where(rank_list == group_index, assignment, 0))
    weight = jnp.sum(jnp.where(rank_list == scenario, probability, 0.0))

    chips = members // 2
    part = selected.shape[0] // members
    mask = bit_of(member, 0) * (selected.shape[0] // 2) + (member >> 1) * part
    place = jnp.stack([member * height, first_row, mask]).astype(jnp.int32)

    def to_chip(block, shift):
        return lax.ppermute(block, "dev", [(i, i ^ (shift << 1)) for i in range(members)])

    def gather_chips(block):
        return jnp.concatenate([block] + [to_chip(block, shift) for shift in range(1, chips)], axis=0)

    keep, away = pick_rows(my_rows, prior_panel, selected, place)
    held = keep + swap(away, "dev", members, 0)
    got = [to_chip(held[shift * part : (shift + 1) * part], shift) for shift in range(1, chips)]
    share = functools.reduce(jnp.add, got, held[:part])
    half = gather_chips(share[:, :wide])
    other = swap(half, "dev", members, 0)
    weight = weight.reshape(1)
    project, summed = make_project(place, weight, inverse_blocks, half, other, share)
    sel8 = jnp.broadcast_to(selected[None, :], (8, selected.shape[0]))

    def orders(lane):
        shift = lane % group_bits
        return [(shift + i) % group_bits for i in range(group_bits)]

    def listing(order, done, flip):
        fixed = group_index ^ (flip << order[done]) if flip else group_index
        settled = done + 1 if flip else done
        free = order[settled:]
        found = []
        for j in range(1 << len(free)):
            value = fixed
            for i, bit in enumerate(free):
                value = (value & ~(1 << bit)) | (((j >> (len(free) - 1 - i)) & 1) << bit)
            found.append(value)
        return found

    def quarter_place(order, settled, quarter):
        index = 0
        for bit in order[settled:]:
            index = 2 * index + bit_of(quarter, bit)
        return index

    def stage_ids(order, stage):
        quarters = listing(order, stage, 1) if stage < group_bits else [group_index]
        ids = list(quarters)
        for earlier in range(stage):
            ids += [quarter_place(order, earlier + 1, quarter) for quarter in quarters]
        return jnp.stack([jnp.asarray(at, jnp.int32) for at in ids])

    gots = [[] for _ in range(lanes)]

    def send_stage(lane, stage, token, held_back=None):
        order = orders(lane)
        ids = after(stage_ids(order, stage), token)
        sent = send_sum(border4, lane, ids, project, weight, gots[lane])
        if held_back is not None:
            sent = after(sent, held_back)
        gots[lane].append(swap(sent, "grp", groups, order[stage]))
        return sent

    def over_group(bit):
        return lambda rows: rows + swap(rows, "grp", groups, bit)

    def over_chips(bit):
        return lambda rows: jnp.concatenate([rows, to_chip(rows, 1 << bit)], axis=0)

    steps = [over_group(bit) for bit in range(group_bits)] + [over_chips(bit) for bit in range(member_bits - 1)]
    token = project
    for lane in range(lanes):
        if lane < len(steps):
            summed = steps[lane](after(summed, token))
        token = send_stage(lane, 0, token, [summed] + ([gots[0][0]] if lane == lanes - 1 > 0 else []))
    for step in steps[lanes:]:
        summed = step(summed)
    corner_half = after(summed, token)
    line = list(range(lanes))
    line[:2] = line[1::-1]
    token = [token, gots[lanes > 1][0]]
    half_way = min(2, lanes)
    for stage in range(1, group_bits):
        for lane in line[:half_way]:
            token = send_stage(lane, stage, token)
            if lane == line[0]:
                corner_half = after(corner_half, token)
    corner_other = swap(corner_half, "dev", members, 0)
    work, prior_sel = start_factor(place, corner_half, after(corner_other, token))
    token = prior_sel
    for stage in range(1, group_bits):
        for lane in line[half_way:]:
            token = send_stage(lane, stage, token)
    inverse_high, inverse_low = finish_factor(after(work, token))
    token = inverse_high
    line = [lane ^ 1 for lane in range(lanes)] if lanes % 2 == 0 else line

    panel_out, early, pending = None, None, []
    near, far = [None] * lanes, [None] * lanes

    def panel_stage(lane, before, held_back, meanwhile=None):
        order = orders(lane)
        first = (first_row + lane * lane_rows).reshape(1).astype(jnp.int32)
        ids = after(stage_ids(order, group_bits), before)
        out, turned = panel_rows(
            border4, lane, ids, project, weight, gots[lane], first,
            prior_panel, prior_sel, inverse_high, inverse_low, sel8, panel_out,
        )
        if meanwhile is not None:
            held_back = held_back + [meanwhile(turned)]
        turned = after(turned, held_back)
        near[lane] = [(turned, group_index, lane)]
        for bit in order:
            near[lane].append((swap(turned, "grp", groups, bit), group_index ^ (1 << bit), lane))
        return out, turned

    def forward(lane, before=()):
        order = orders(lane)
        far[lane] = []
        layer = [((after(block, before), at, lane), i) for i, (block, at, _) in enumerate(near[lane][1:])]
        while layer:
            following = []
            for (block, at, _), i in layer:
                for k in range(i + 1, len(order)):
                    piece = (swap(block, "grp", groups, order[k]), at ^ (1 << order[k]), lane)
                    far[lane].append(piece)
                    following.append((piece, k))
            layer = following

    def blocks_of(pieces):
        return [block for block, _, _ in pieces]

    def add_up(pieces, before, total):
        return residual_add(border4, members, [(after(block, before), at, lane) for block, at, lane in pieces], total)

    def arrived(lane):
        return blocks_of(near[lane][1:])

    for turn, lane in enumerate(line):
        before, held_back, meanwhile = [token], [], None
        if turn == 1:
            held_back = [gots[other][-1] for other in line[2:]]
        if turn == 2:
            held_back = arrived(line[0])
            forward(line[0])
        if turn >= 3:
            before = before + arrived(line[turn - 2])
            forward(line[turn - 2])
            held_back = arrived(line[turn - 1]) + blocks_of(far[line[turn - 3]] + far[line[turn - 2]])

            def meanwhile(raw):
                nonlocal early
                early = add_up(near[line[turn - 2]], raw, early)
                return early

        panel_out, token = panel_stage(lane, before, held_back, meanwhile)
        if turn == 2:
            early = add_up(near[line[0]], token, early)
            token = early
    forward(line[-2])
    early = add_up([piece for lane in line[:-2] for piece in far[lane]] + near[line[-2]], token, early)
    forward(line[-1], early)
    early = add_up(near[line[-1]], early, early)
    total = residual_add(border4, members, far[line[-2]] + far[line[-1]], early)

    core, chip = bit_of(member, 0), member >> 1

    def sum_cores(total):
        held = total.reshape((chips, 2) + total.shape[1:])
        away = lax.dynamic_index_in_dim(held, 1 - core, 1, keepdims=False)
        return lax.dynamic_index_in_dim(held, core, 1, keepdims=False), swap(away, "dev", members, 0)

    def sum_chips(held):
        return [to_chip(lax.dynamic_index_in_dim(held, chip ^ shift, 0, keepdims=False), shift) for shift in range(1, chips)]

    held, coded = code_sum(*sum_cores(total))
    result = lax.dynamic_index_in_dim(held, chip, 0, keepdims=False)
    for got in sum_chips(coded):
        result = result + got[:cols].astype(F32) * jnp.exp2(got[cols : cols + 1].astype(F32))
    residual = result.T / math.sqrt(N1)
    return (panel_out, residual[None])


def solution(mesh):
    return jax.shard_map(
        body,
        mesh=mesh,
        in_specs=(
            P("grp", "dev", None),
            P("grp", None, None),
            P(),
            P(),
            P(),
            P(("dev", "grp"), None),
        ),
        out_specs=(P(("dev", "grp"), None), P("grp", "dev", None)),
        check_vma=False,
    )
```

```python
import functools
import math

import jax
import jax.numpy as jnp
from jax import lax
from jax.experimental import pallas as pl
from jax.experimental.pallas import tpu as pltpu
from jax.sharding import PartitionSpec as P

N1 = 131072
LANES = 4
EXTRA = 16
TILE_BITS = 4
PIVOTS = 4
STEP = 512
EXACT = lax.Precision.HIGHEST
HBM = pltpu.HBM
VMEM = 60 * 1024 * 1024
VMEM_SOME = 32 * 1024 * 1024
SMALL = pl.CostEstimate(flops=1 << 16, bytes_accessed=1 << 12, transcendentals=0)
F32, BF16 = jnp.float32, jnp.bfloat16


def swap(value, axis, size, bit):
    return lax.ppermute(value, axis, [(i, i ^ (1 << bit)) for i in range(size)])


def after(value, done):
    return lax.optimization_barrier((value, done))[0]


def bit_of(index, bit):
    return (index >> bit) & 1


def pick_kernel(place_ref, sel_ref, border_ref, prior_ref, keep_ref, away_ref, btile, ptile, rows, names, sems):
    count = sel_ref.shape[0]
    wide = border_ref.shape[1]
    height, own = border_ref.shape[0], prior_ref.shape[0]
    b_first, p_first, mask = place_ref[0], place_ref[1], place_ref[2]
    tile_rows = 1 << TILE_BITS

    def scan(j, found):
        offset = sel_ref[j] - b_first
        names[found] = j
        return found + ((offset >= 0) & (offset < height)).astype(jnp.int32)

    found = lax.fori_loop(0, count, scan, jnp.int32(0), unroll=16)

    def copies(i):
        at = sel_ref[names[i]]
        b_off, p_off = at - b_first, at - p_first
        p_in = (p_off >= 0) & (p_off < own)
        p_off = jnp.clip(p_off, 0, own - 1)
        b_base = pl.multiple_of((b_off >> TILE_BITS) << TILE_BITS, tile_rows)
        p_base = pl.multiple_of((p_off >> TILE_BITS) << TILE_BITS, tile_rows)
        b_copy = pltpu.make_async_copy(border_ref.at[pl.ds(b_base, tile_rows)], btile.at[i], sems.at[0])
        p_copy = pltpu.make_async_copy(prior_ref.at[pl.ds(p_base, tile_rows)], ptile.at[i], sems.at[1])
        return b_copy, p_copy, p_in, b_off - b_base, p_off - p_base

    def start(i, carry):
        b_copy, p_copy, p_in, _, _ = copies(i)
        b_copy.start()
        pl.when(p_in)(p_copy.start)
        return carry

    def wait(i, carry):
        b_copy, p_copy, p_in, _, _ = copies(i)
        b_copy.wait()
        pl.when(p_in)(p_copy.wait)
        return carry

    def place_four(q, carry):
        for u in range(4):
            i = jnp.minimum(4 * q + u, found - 1)
            _, _, p_in, b_row, p_row = copies(i)
            at = names[i] ^ mask
            ids = lax.broadcasted_iota(jnp.int32, btile.shape[1:], 0)
            row = jnp.where(ids == b_row, btile[i].astype(F32), 0.0)
            rows[pl.ds(at, 1), :wide] = jnp.sum(row, axis=0, keepdims=True)
            ids = lax.broadcasted_iota(jnp.int32, ptile.shape[1:], 0)
            row = jnp.where((ids == p_row) & p_in, ptile[i].astype(F32), 0.0)
            rows[pl.ds(at, 1), wide:] = jnp.sum(row, axis=0, keepdims=True)
        return carry

    lax.fori_loop(0, found, start, 0)
    rows[...] = jnp.zeros_like(rows)
    lax.fori_loop(0, found, wait, 0)
    lax.fori_loop(0, (found + 3) >> 2, place_four, 0)
    keep_ref[...] = rows[: count // 2, :].astype(BF16)
    away_ref[...] = rows[count // 2 :, :].astype(BF16)


def pick_rows(my_rows, prior_panel, selected, place):
    count = selected.shape[0]
    wide, narrow = my_rows.shape[1], prior_panel.shape[1]
    return pl.pallas_call(
        pick_kernel,
        out_shape=[jax.ShapeDtypeStruct((count // 2, wide + narrow), BF16)] * 2,
        in_specs=[
            pl.BlockSpec(memory_space=pltpu.SMEM),
            pl.BlockSpec(memory_space=pltpu.SMEM),
            pl.BlockSpec(memory_space=pl.ANY),
            pl.BlockSpec(memory_space=pl.ANY),
        ],
        out_specs=[pl.BlockSpec(memory_space=pltpu.VMEM)] * 2,
        scratch_shapes=[
            pltpu.VMEM((count, 1 << TILE_BITS, wide), BF16),
            pltpu.VMEM((count, 1 << TILE_BITS, narrow), BF16),
            pltpu.VMEM((count, wide + narrow), F32),
            pltpu.SMEM((count,), jnp.int32),
            pltpu.SemaphoreType.DMA((2,)),
        ],
        compiler_params=pltpu.CompilerParams(vmem_limit_bytes=VMEM),
        cost_estimate=SMALL,
        name="pick_rows",
    )(place, selected, my_rows, prior_panel)


def place_matrix(mask, count, dtype):
    place = lax.broadcasted_iota(jnp.int32, (count, count), 0)
    column = lax.broadcasted_iota(jnp.int32, (count, count), 1)
    return jnp.where((column ^ mask) == place, 1.0, 0.0).astype(dtype)


def project_kernel(place_ref, weight_ref, inverse_ref, half_ref, other_ref, share_ref, project_ref, payload_ref):
    count = project_ref.shape[1]
    wide = half_ref.shape[1]

    def times(rows):
        return lax.dot_general(inverse_ref[0], rows, (((1,), (1,)), ((), ())), preferred_element_type=F32).astype(BF16)

    placed = jnp.concatenate([times(half_ref[...]), times(other_ref[...])], axis=1)
    project = jnp.dot(placed, place_matrix(place_ref[2], count, BF16), preferred_element_type=F32).astype(BF16)
    project_ref[...] = project
    payload_ref[:, :count] = weight_ref[0] * jnp.dot(share_ref[:, :wide], project, preferred_element_type=F32)
    payload_ref[:, count:] = share_ref[:, wide:].astype(F32)


def make_project(place, weight, inverse_blocks, half, other, share):
    wide = inverse_blocks.shape[1]
    count = 2 * half.shape[0]
    part = share.shape[0]
    vmem = pl.BlockSpec(memory_space=pltpu.VMEM)
    smem = pl.BlockSpec(memory_space=pltpu.SMEM)
    return pl.pallas_call(
        project_kernel,
        in_specs=[smem, smem, vmem, vmem, vmem, vmem],
        out_specs=[vmem, vmem],
        out_shape=[jax.ShapeDtypeStruct((wide, count), BF16), jax.ShapeDtypeStruct((part, 2 * count), F32)],
        compiler_params=pltpu.CompilerParams(vmem_limit_bytes=VMEM_SOME),
        cost_estimate=SMALL,
        name="make_project",
    )(place, weight, inverse_blocks, half, other, share)


def chunk_copies(lane, parts, ids_ref, border_ref, held, sem, got_refs, got_held, got_sems):
    step = held.shape[1]
    blocks = held.shape[0] // parts
    copies, got_copies = [], [[] for _ in got_refs]
    for j in range(parts):
        for t in range(blocks):
            slot = j * blocks + t
            source = border_ref.at[ids_ref[j], lane, pl.ds(t * step, step)]
            copies.append(pltpu.make_async_copy(source, held.at[slot], sem.at[slot]))
            for g, got_ref in enumerate(got_refs):
                source = got_ref.at[ids_ref[parts * (g + 1) + j], t]
                got_copies[g].append(pltpu.make_async_copy(source, got_held[g].at[slot], got_sems[g].at[slot]))
    for slot in range(len(copies)):
        copies[slot].start()
        for one in got_copies:
            one[slot].start()
    return copies, list(zip(got_copies, got_held))


def send_kernel(lane, parts, gots, ids_ref, border_ref, project_ref, weight_ref, *refs):
    got_refs, out_ref = refs[:gots], refs[gots]
    scratch = refs[gots + 1 :]
    held, sem, got_held, got_sems = scratch[0], scratch[1], scratch[2 : 2 + gots], scratch[2 + gots :]
    copies, incoming = chunk_copies(lane, parts, ids_ref, border_ref, held, sem, got_refs, got_held, got_sems)
    blocks = held.shape[0] // parts
    for slot in range(len(copies)):
        copies[slot].wait()
        total = jnp.dot(held[slot], project_ref[...], preferred_element_type=F32) * weight_ref[0]
        rows, cols = total.shape
        for got_copies, got in incoming:
            got_copies[slot].wait()
            power = got[slot, rows : rows + EXTRA, :].astype(F32)[0:1, :]
            total = total + got[slot, :rows, :].astype(F32) * jnp.exp2(power)
        largest = jnp.maximum(jnp.max(jnp.abs(total), axis=0, keepdims=True), 1e-30)
        power = jnp.ceil(jnp.log2(largest)) - 15.0
        whole = jnp.clip(jnp.round(total * jnp.exp2(-power)), -32767.0, 32767.0)
        out_ref[slot // blocks, slot % blocks, :rows, :] = whole.astype(jnp.int32).astype(jnp.int16)
        out_ref[slot // blocks, slot % blocks, rows:, :] = (
            jnp.broadcast_to(power, (EXTRA, cols)).astype(jnp.int32).astype(jnp.int16)
        )


def chunk_scratch(slots, step, wide, cols, gots):
    shapes = [pltpu.VMEM((slots, step, wide), BF16), pltpu.SemaphoreType.DMA((slots,))]
    shapes += [pltpu.VMEM((slots, step + EXTRA, cols), jnp.int16)] * gots
    return shapes + [pltpu.SemaphoreType.DMA((slots,))] * gots


def send_sum(border4, lane, ids, project, weight, gots):
    _, _, rows, wide = border4.shape
    cols = project.shape[1]
    parts = ids.shape[0] // (len(gots) + 1)
    step = min(rows, STEP)
    blocks = rows // step
    vmem = pl.BlockSpec(memory_space=pltpu.VMEM)
    smem = pl.BlockSpec(memory_space=pltpu.SMEM)
    hbm = pl.BlockSpec(memory_space=HBM)
    return pl.pallas_call(
        functools.partial(send_kernel, lane, parts, len(gots)),
        in_specs=[smem, hbm, vmem, smem] + [hbm] * len(gots),
        out_specs=vmem,
        out_shape=jax.ShapeDtypeStruct((parts, blocks, step + EXTRA, cols), jnp.int16),
        scratch_shapes=chunk_scratch(parts * blocks, step, wide, cols, len(gots)),
        compiler_params=pltpu.CompilerParams(vmem_limit_bytes=VMEM_SOME),
        cost_estimate=pl.CostEstimate(flops=1 << 16, bytes_accessed=12 << 20, transcendentals=0),
        name="send_sum",
    )(ids, border4, project, weight, *gots)


def factor_start(place_ref, half_ref, other_ref, work_ref, prior_ref):
    count = 2 * half_ref.shape[0]
    turn = place_matrix(place_ref[2], count, F32)

    def placed(columns):
        rows = jnp.concatenate([half_ref[:, columns], other_ref[:, columns]], axis=0)
        return lax.dot_general(turn, rows, (((0,), (0,)), ((), ())), preferred_element_type=F32, precision=EXACT)

    prior_sel = placed(slice(count, 2 * count)).astype(BF16)
    prior_ref[...] = prior_sel
    corner = placed(slice(0, count)) - lax.dot_general(
        prior_sel, prior_sel, (((1,), (1,)), ((), ())), preferred_element_type=F32
    )
    work_ref[:, :count] = 0.5 * (corner + corner.T)
    work_ref[:, count:] = jnp.where(
        lax.broadcasted_iota(jnp.int32, (count, count), 0) == lax.broadcasted_iota(jnp.int32, (count, count), 1), 1.0, 0.0
    )
    factor_blocks(work_ref, 0, 2)


def factor_finish(before_ref, high_ref, low_ref, work):
    count = before_ref.shape[0]
    work[...] = before_ref[...]
    factor_blocks(work, 2, 4)
    inverse = work[:, count:]
    top = inverse.astype(BF16)
    high_ref[...] = top
    low_ref[...] = (inverse - top.astype(F32)).astype(BF16)


def factor_blocks(work, begin, end):
    count = work.shape[0]
    side = count // 4
    for k in range(begin, end):
        low, high = k * side, (k + 1) * side
        same = jnp.where(
            lax.broadcasted_iota(jnp.int32, (side, side), 0) == lax.broadcasted_iota(jnp.int32, (side, side), 1), 1.0, 0.0
        )
        tiles = jnp.concatenate([work[low:high, low:high], same], axis=1)
        tiles = [tiles[8 * i : 8 * i + 8, :] for i in range(side // 8)]
        row_ids = lax.broadcasted_iota(jnp.int32, tiles[0].shape, 0)
        for j in range(0, side, PIVOTS):
            home, inner = j // 8, j % 8
            lanes = tiles[0].shape[1]
            columns = [
                [jnp.broadcast_to(tile[:, j + q : j + q + 1], tile.shape) for tile in tiles[home:]] for q in range(PIVOTS)
            ]
            rows = [tiles[home][inner + q : inner + q + 1, :] for q in range(PIVOTS)]
            for q in range(PIVOTS):
                pivot = columns[q][0][inner + q : inner + q + 1, :]
                scale = lax.rsqrt(pivot)
                scale = scale * (1.5 - 0.5 * pivot * scale * scale)
                rows[q] = rows[q] * scale
                columns[q] = [column * scale for column in columns[q]]
                for r in range(q + 1, PIVOTS):
                    entry = columns[q][0][inner + r : inner + r + 1, :]
                    rows[r] = rows[r] - entry * rows[q]
                    columns[r] = [a - entry * b for a, b in zip(columns[r], columns[q])]
            for i in range(home, side // 8):
                new = tiles[i]
                for q in range(PIVOTS):
                    new = new - columns[q][i - home] * rows[q]
                if i == home:
                    new = jnp.where(row_ids >= inner + PIVOTS, new, tiles[i])
                    for q in range(PIVOTS):
                        new = jnp.where(row_ids == inner + q, rows[q], new)
                tiles[i] = new
        inverse = jnp.concatenate([tile[:, side:] for tile in tiles], axis=0)
        block = jnp.dot(inverse, work[low:high, :], preferred_element_type=F32, precision=EXACT)
        work[low:high, :] = block
        if high < count:
            work[high:, :] = work[high:, :] - lax.dot_general(
                block[:, high:count], block, (((0,), (0,)), ((), ())), preferred_element_type=F32, precision=EXACT
            )

def factor_call(kernel, shapes, args, scratch=()):
    vmem = pl.BlockSpec(memory_space=pltpu.VMEM)
    smem = pl.BlockSpec(memory_space=pltpu.SMEM)
    return pl.pallas_call(
        kernel,
        in_specs=[smem if arg.ndim == 1 else vmem for arg in args],
        out_specs=[vmem] * len(shapes),
        out_shape=shapes,
        scratch_shapes=list(scratch),
        compiler_params=pltpu.CompilerParams(vmem_limit_bytes=VMEM_SOME),
        cost_estimate=SMALL,
        name=kernel.__name__,
    )(*args)


def start_factor(place, half, other):
    count = 2 * half.shape[0]
    shapes = [jax.ShapeDtypeStruct((count, 2 * count), F32), jax.ShapeDtypeStruct((count, count), BF16)]
    return factor_call(factor_start, shapes, [place, half, other])


def finish_factor(work):
    count = work.shape[0]
    shapes = [jax.ShapeDtypeStruct((count, count), BF16)] * 2
    return factor_call(factor_finish, shapes, [work], [pltpu.VMEM(work.shape, F32)])


def panel_kernel(lane, gots, aliased, ids_ref, border_ref, project_ref, weight_ref, *refs):
    got_refs, refs = refs[:gots], refs[gots:]
    first_ref, prior_ref, prior_sel_ref, high_ref, low_ref, sel_ref = refs[:6]
    out_ref, turned_ref = refs[6 + aliased : 8 + aliased]
    scratch = refs[8 + aliased :]
    held, sem, got_held, got_sems = scratch[0], scratch[1], scratch[2 : 2 + gots], scratch[2 + gots :]
    copies, incoming = chunk_copies(lane, 1, ids_ref, border_ref, held, sem, got_refs, got_held, got_sems)

    def times(a, b):
        return lax.dot_general(a, b, (((1,), (1,)), ((), ())), preferred_element_type=F32)

    for slot in range(len(copies)):
        rows = held.shape[1]
        here = slice(slot * rows, (slot + 1) * rows)
        copies[slot].wait()
        total = jnp.dot(held[slot], project_ref[...], preferred_element_type=F32) * weight_ref[0]
        total = total - times(prior_ref[here, :], prior_sel_ref[...])
        for got_copies, got in incoming:
            got_copies[slot].wait()
            power = got[slot, rows : rows + EXTRA, :].astype(F32)[0:1, :]
            total = total + got[slot, :rows, :].astype(F32) * jnp.exp2(power)
        high = total.astype(BF16)
        low = (total - high.astype(F32)).astype(BF16)
        solved = times(high, high_ref[...]) + (times(low, high_ref[...]) + times(high, low_ref[...]))
        ids = first_ref[0] + slot * rows + lax.broadcasted_iota(jnp.int32, (rows, 1), 0)
        hits = jnp.where(ids == sel_ref[0:1, :], 1.0, 0.0)
        marked = jnp.max(hits, axis=1, keepdims=True)
        solved = jnp.where(marked > 0.0, 0.0, solved)
        out_ref[here, :] = solved
        turned_ref[:, here] = jnp.transpose(solved.astype(BF16))


def panel_rows(border4, lane, ids, project, weight, gots, first, prior_panel, prior_sel, high, low, sel8, done):
    _, lanes, rows, wide = border4.shape
    own, cols = prior_panel.shape
    step = min(rows, STEP)
    vmem = pl.BlockSpec(memory_space=pltpu.VMEM)
    smem = pl.BlockSpec(memory_space=pltpu.SMEM)
    hbm = pl.BlockSpec(memory_space=HBM)
    mine = pl.BlockSpec((rows, cols), lambda t: (lane, 0))
    in_specs = [smem, hbm, vmem, smem] + [hbm] * len(gots) + [smem, mine, vmem, vmem, vmem, vmem]
    args = [ids, border4, project, weight, *gots, first, prior_panel, prior_sel, high, low, sel8]
    aliases = {}
    if done is not None:
        in_specs.append(hbm)
        args.append(done)
        aliases = {len(args) - 1: 0}
    return pl.pallas_call(
        functools.partial(panel_kernel, lane, len(gots), len(aliases)),
        grid=(1,),
        in_specs=in_specs,
        out_specs=[mine, vmem],
        out_shape=[jax.ShapeDtypeStruct((own, cols), F32), jax.ShapeDtypeStruct((cols, rows), BF16)],
        input_output_aliases=aliases,
        scratch_shapes=chunk_scratch(rows // step, step, wide, cols, len(gots)),
        compiler_params=pltpu.CompilerParams(vmem_limit_bytes=VMEM_SOME),
        cost_estimate=pl.CostEstimate(flops=1 << 16, bytes_accessed=16 << 20, transcendentals=0),
        name="panel_rows",
    )(*args)


def residual_kernel(lanes, ids_ref, border_ref, *refs):
    parts = len(lanes)
    pieces, out_ref, held, sems, turned, turned_sems = refs[:parts], *refs[-5:]
    before = None
    if len(refs) > parts + 5:
        before = pltpu.make_async_copy(refs[parts], out_ref, turned_sems.at[parts])
        before.start()
    members, _, block = out_ref.shape
    step = held.shape[1]
    blocks = turned.shape[2] // step
    copies, turned_copies = [], []
    for j in range(parts):
        turned_copies.append(pltpu.make_async_copy(pieces[j], turned.at[j], turned_sems.at[j]))
        turned_copies[j].start()
        for t in range(blocks):
            slot = j * blocks + t
            source = border_ref.at[ids_ref[j], lanes[j], pl.ds(t * step, step)]
            copies.append(pltpu.make_async_copy(source, held.at[slot], sems.at[slot]))
            copies[slot].start()
    for slot, copy in enumerate(copies):
        j, t = slot // blocks, slot % blocks
        if t == 0:
            turned_copies[j].wait()
        copy.wait()
        if slot == 0 and before is not None:
            before.wait()
        product = jnp.dot(turned[j][:, t * step : (t + 1) * step], held[slot], preferred_element_type=F32)
        for m in range(members):
            here = product[:, m * block : (m + 1) * block]
            if slot > 0 or before is not None:
                out_ref[m] += here
            else:
                out_ref[m] = here


def residual_add(border4, members, pieces, total):
    _, _, rows, wide = border4.shape
    cols = pieces[0][0].shape[0]
    parts = len(pieces)
    step = min(rows, STEP)
    slots = parts * (rows // step)
    ids = jnp.stack([at for _, at, _ in pieces]).astype(jnp.int32)
    vmem = pl.BlockSpec(memory_space=pltpu.VMEM)
    args = [ids, border4] + [block for block, _, _ in pieces]
    if total is not None:
        args.append(total)
    return pl.pallas_call(
        functools.partial(residual_kernel, [lane for _, _, lane in pieces]),
        in_specs=[pl.BlockSpec(memory_space=pltpu.SMEM)] + [pl.BlockSpec(memory_space=HBM)] * (len(args) - 1),
        out_specs=vmem,
        out_shape=jax.ShapeDtypeStruct((members, cols, wide // members), F32),
        scratch_shapes=[
            pltpu.VMEM((slots, step, wide), BF16),
            pltpu.SemaphoreType.DMA((slots,)),
            pltpu.VMEM((parts, cols, rows), BF16),
            pltpu.SemaphoreType.DMA((parts + 1,)),
        ],
        compiler_params=pltpu.CompilerParams(vmem_limit_bytes=VMEM_SOME),
        cost_estimate=pl.CostEstimate(flops=1 << 16, bytes_accessed=12 << 20, transcendentals=0),
        name="residual_add",
    )(*args)


def code_kernel(kept_ref, got_ref, sum_ref, coded_ref):
    rows, cols = kept_ref.shape[1:]
    for chip in range(kept_ref.shape[0]):
        total = kept_ref[chip] + got_ref[chip]
        sum_ref[chip] = total
        largest = jnp.maximum(jnp.max(jnp.abs(total), axis=0, keepdims=True), 1e-30)
        power = jnp.ceil(jnp.log2(largest)) - 15.0
        whole = jnp.clip(jnp.round(total * jnp.exp2(-power)), -32767.0, 32767.0)
        coded_ref[chip, :rows, :] = whole.astype(jnp.int32).astype(jnp.int16)
        coded_ref[chip, rows:, :] = jnp.broadcast_to(power, (EXTRA, cols)).astype(jnp.int32).astype(jnp.int16)


def code_sum(kept, got):
    chips, rows, cols = kept.shape
    vmem = pl.BlockSpec(memory_space=pltpu.VMEM)
    return pl.pallas_call(
        code_kernel,
        in_specs=[vmem, vmem],
        out_specs=[vmem, vmem],
        out_shape=[
            jax.ShapeDtypeStruct((chips, rows, cols), F32),
            jax.ShapeDtypeStruct((chips, rows + EXTRA, cols), jnp.int16),
        ],
        compiler_params=pltpu.CompilerParams(vmem_limit_bytes=VMEM_SOME),
        cost_estimate=SMALL,
        name="code_sum",
    )(kept, got)


def body(border, inverse_blocks, selected, assignment, probability, prior_panel):
    groups = lax.axis_size("grp")
    members = lax.axis_size("dev")
    group_index = lax.axis_index("grp")
    member = lax.axis_index("dev")
    group_bits = groups.bit_length() - 1
    member_bits = members.bit_length() - 1
    my_rows = border[0]
    height, wide = my_rows.shape
    own_rows, cols = prior_panel.shape
    lanes = min(LANES, own_rows // 128)
    lane_rows = own_rows // lanes
    border4 = my_rows.reshape(groups, lanes, lane_rows, wide)
    first_row = (member * groups + group_index) * own_rows

    rank_list = jnp.arange(groups, dtype=jnp.int32)
    scenario = jnp.sum(jnp.where(rank_list == group_index, assignment, 0))
    weight = jnp.sum(jnp.where(rank_list == scenario, probability, 0.0))

    chips = members // 2
    part = selected.shape[0] // members
    mask = bit_of(member, 0) * (selected.shape[0] // 2) + (member >> 1) * part
    place = jnp.stack([member * height, first_row, mask]).astype(jnp.int32)

    def to_chip(block, shift):
        return lax.ppermute(block, "dev", [(i, i ^ (shift << 1)) for i in range(members)])

    def gather_chips(block):
        return jnp.concatenate([block] + [to_chip(block, shift) for shift in range(1, chips)], axis=0)

    keep, away = pick_rows(my_rows, prior_panel, selected, place)
    held = keep + swap(away, "dev", members, 0)
    got = [to_chip(held[shift * part : (shift + 1) * part], shift) for shift in range(1, chips)]
    share = functools.reduce(jnp.add, got, held[:part])
    half = gather_chips(share[:, :wide])
    other = swap(half, "dev", members, 0)
    weight = weight.reshape(1)
    project, summed = make_project(place, weight, inverse_blocks, half, other, share)
    sel8 = jnp.broadcast_to(selected[None, :], (8, selected.shape[0]))

    def orders(lane):
        shift = lane % group_bits
        return [(shift + i) % group_bits for i in range(group_bits)]

    def listing(order, done, flip):
        fixed = group_index ^ (flip << order[done]) if flip else group_index
        settled = done + 1 if flip else done
        free = order[settled:]
        found = []
        for j in range(1 << len(free)):
            value = fixed
            for i, bit in enumerate(free):
                value = (value & ~(1 << bit)) | (((j >> (len(free) - 1 - i)) & 1) << bit)
            found.append(value)
        return found

    def quarter_place(order, settled, quarter):
        index = 0
        for bit in order[settled:]:
            index = 2 * index + bit_of(quarter, bit)
        return index

    def stage_ids(order, stage):
        quarters = listing(order, stage, 1) if stage < group_bits else [group_index]
        ids = list(quarters)
        for earlier in range(stage):
            ids += [quarter_place(order, earlier + 1, quarter) for quarter in quarters]
        return jnp.stack([jnp.asarray(at, jnp.int32) for at in ids])

    gots = [[] for _ in range(lanes)]

    def send_stage(lane, stage, token, held_back=None):
        order = orders(lane)
        ids = after(stage_ids(order, stage), token)
        sent = send_sum(border4, lane, ids, project, weight, gots[lane])
        if held_back is not None:
            sent = after(sent, held_back)
        gots[lane].append(swap(sent, "grp", groups, order[stage]))
        return sent

    def over_group(bit):
        return lambda rows: rows + swap(rows, "grp", groups, bit)

    def over_chips(bit):
        return lambda rows: jnp.concatenate([rows, to_chip(rows, 1 << bit)], axis=0)

    steps = [over_group(bit) for bit in range(group_bits)] + [over_chips(bit) for bit in range(member_bits - 1)]
    token = project
    for lane in range(lanes):
        if lane < len(steps):
            summed = steps[lane](after(summed, token))
        token = send_stage(lane, 0, token, [summed] + ([gots[0][0]] if lane == lanes - 1 > 0 else []))
    for step in steps[lanes:]:
        summed = step(summed)
    corner_half = after(summed, token)
    line = list(range(lanes))
    line[:2] = line[1::-1]
    token = [token, gots[lanes > 1][0]]
    half_way = min(2, lanes)
    for stage in range(1, group_bits):
        for lane in line[:half_way]:
            token = send_stage(lane, stage, token)
            if lane == line[0]:
                corner_half = after(corner_half, token)
    corner_other = swap(corner_half, "dev", members, 0)
    work, prior_sel = start_factor(place, corner_half, after(corner_other, token))
    token = prior_sel
    for stage in range(1, group_bits):
        for lane in line[half_way:]:
            token = send_stage(lane, stage, token)
    inverse_high, inverse_low = finish_factor(after(work, token))
    token = inverse_high
    line = [lane ^ 1 for lane in range(lanes)] if lanes % 2 == 0 else line

    panel_out, early, pending = None, None, []
    near, far = [None] * lanes, [None] * lanes

    def panel_stage(lane, before, held_back, meanwhile=None):
        order = orders(lane)
        first = (first_row + lane * lane_rows).reshape(1).astype(jnp.int32)
        ids = after(stage_ids(order, group_bits), before)
        out, turned = panel_rows(
            border4, lane, ids, project, weight, gots[lane], first,
            prior_panel, prior_sel, inverse_high, inverse_low, sel8, panel_out,
        )
        if meanwhile is not None:
            held_back = held_back + [meanwhile(turned)]
        turned = after(turned, held_back)
        near[lane] = [(turned, group_index, lane)]
        for bit in order:
            near[lane].append((swap(turned, "grp", groups, bit), group_index ^ (1 << bit), lane))
        return out, turned

    def forward(lane, before=()):
        order = orders(lane)
        far[lane] = []
        layer = [((after(block, before), at, lane), i) for i, (block, at, _) in enumerate(near[lane][1:])]
        while layer:
            following = []
            for (block, at, _), i in layer:
                for k in range(i + 1, len(order)):
                    piece = (swap(block, "grp", groups, order[k]), at ^ (1 << order[k]), lane)
                    far[lane].append(piece)
                    following.append((piece, k))
            layer = following

    def blocks_of(pieces):
        return [block for block, _, _ in pieces]

    def add_up(pieces, before, total):
        return residual_add(border4, members, [(after(block, before), at, lane) for block, at, lane in pieces], total)

    def arrived(lane):
        return blocks_of(near[lane][1:])

    for turn, lane in enumerate(line):
        before, held_back, meanwhile = [token], [], None
        if turn == 1:
            held_back = [gots[other][-1] for other in line[2:]]
        if turn == 2:
            held_back = arrived(line[0])
            forward(line[0])
        if turn >= 3:
            before = before + arrived(line[turn - 2])
            forward(line[turn - 2])
            held_back = arrived(line[turn - 1]) + blocks_of(far[line[turn - 3]] + far[line[turn - 2]])

            def meanwhile(raw):
                nonlocal early
                early = add_up(near[line[turn - 2]], raw, early)
                return early

        panel_out, token = panel_stage(lane, before, held_back, meanwhile)
        if turn == 2:
            early = add_up(near[line[0]], token, early)
            token = early
    forward(line[-2])
    early = add_up([piece for lane in line[:-2] for piece in far[lane]] + near[line[-2]], token, early)
    forward(line[-1], early)
    early = add_up(near[line[-1]], early, early)
    total = residual_add(border4, members, far[line[-2]] + far[line[-1]], early)

    core, chip = bit_of(member, 0), member >> 1

    def sum_cores(total):
        held = total.reshape((chips, 2) + total.shape[1:])
        away = lax.dynamic_index_in_dim(held, 1 - core, 1, keepdims=False)
        return lax.dynamic_index_in_dim(held, core, 1, keepdims=False), swap(away, "dev", members, 0)

    def sum_chips(held):
        return [to_chip(lax.dynamic_index_in_dim(held, chip ^ shift, 0, keepdims=False), shift) for shift in range(1, chips)]

    held, coded = code_sum(*sum_cores(total))
    result = lax.dynamic_index_in_dim(held, chip, 0, keepdims=False)
    for got in sum_chips(coded):
        result = result + got[:cols].astype(F32) * jnp.exp2(got[cols : cols + 1].astype(F32))
    residual = result.T / math.sqrt(N1)
    return (panel_out, residual[None])


def solution(mesh):
    return jax.shard_map(
        body,
        mesh=mesh,
        in_specs=(
            P("grp", "dev", None),
            P("grp", None, None),
            P(),
            P(),
            P(),
            P(("dev", "grp"), None),
        ),
        out_specs=(P(("dev", "grp"), None), P("grp", "dev", None)),
        check_vma=False,
    )
```

```python
import functools
import math

import jax
import jax.numpy as jnp
from jax import lax
from jax.experimental import pallas as pl
from jax.experimental.pallas import tpu as pltpu
from jax.sharding import PartitionSpec as P

N1 = 131072
LANES = 4
EXTRA = 16
TILE_BITS = 4
PIVOTS = 4
STEP = 1024
EXACT = lax.Precision.HIGHEST
HBM = pltpu.HBM
VMEM = 60 * 1024 * 1024
VMEM_SOME = 32 * 1024 * 1024
SMALL = pl.CostEstimate(flops=1 << 16, bytes_accessed=1 << 12, transcendentals=0)
F32, BF16 = jnp.float32, jnp.bfloat16


def swap(value, axis, size, bit):
    return lax.ppermute(value, axis, [(i, i ^ (1 << bit)) for i in range(size)])


def after(value, done):
    return lax.optimization_barrier((value, done))[0]


def bit_of(index, bit):
    return (index >> bit) & 1


def pick_kernel(place_ref, sel_ref, border_ref, prior_ref, keep_ref, away_ref, btile, ptile, rows, names, sems):
    count = sel_ref.shape[0]
    wide = border_ref.shape[1]
    height, own = border_ref.shape[0], prior_ref.shape[0]
    b_first, p_first, mask = place_ref[0], place_ref[1], place_ref[2]
    tile_rows = 1 << TILE_BITS

    def scan(j, found):
        offset = sel_ref[j] - b_first
        names[found] = j
        return found + ((offset >= 0) & (offset < height)).astype(jnp.int32)

    found = lax.fori_loop(0, count, scan, jnp.int32(0), unroll=16)

    def copies(i):
        at = sel_ref[names[i]]
        b_off, p_off = at - b_first, at - p_first
        p_in = (p_off >= 0) & (p_off < own)
        p_off = jnp.clip(p_off, 0, own - 1)
        b_base = pl.multiple_of((b_off >> TILE_BITS) << TILE_BITS, tile_rows)
        p_base = pl.multiple_of((p_off >> TILE_BITS) << TILE_BITS, tile_rows)
        b_copy = pltpu.make_async_copy(border_ref.at[pl.ds(b_base, tile_rows)], btile.at[i], sems.at[0])
        p_copy = pltpu.make_async_copy(prior_ref.at[pl.ds(p_base, tile_rows)], ptile.at[i], sems.at[1])
        return b_copy, p_copy, p_in, b_off - b_base, p_off - p_base

    def start(i, carry):
        b_copy, p_copy, p_in, _, _ = copies(i)
        b_copy.start()
        pl.when(p_in)(p_copy.start)
        return carry

    def wait(i, carry):
        b_copy, p_copy, p_in, _, _ = copies(i)
        b_copy.wait()
        pl.when(p_in)(p_copy.wait)
        return carry

    def place_four(q, carry):
        for u in range(4):
            i = jnp.minimum(4 * q + u, found - 1)
            _, _, p_in, b_row, p_row = copies(i)
            at = names[i] ^ mask
            ids = lax.broadcasted_iota(jnp.int32, btile.shape[1:], 0)
            row = jnp.where(ids == b_row, btile[i].astype(F32), 0.0)
            rows[pl.ds(at, 1), :wide] = jnp.sum(row, axis=0, keepdims=True)
            ids = lax.broadcasted_iota(jnp.int32, ptile.shape[1:], 0)
            row = jnp.where((ids == p_row) & p_in, ptile[i].astype(F32), 0.0)
            rows[pl.ds(at, 1), wide:] = jnp.sum(row, axis=0, keepdims=True)
        return carry

    lax.fori_loop(0, found, start, 0)
    rows[...] = jnp.zeros_like(rows)
    lax.fori_loop(0, found, wait, 0)
    lax.fori_loop(0, (found + 3) >> 2, place_four, 0)
    keep_ref[...] = rows[: count // 2, :].astype(BF16)
    away_ref[...] = rows[count // 2 :, :].astype(BF16)


def pick_rows(my_rows, prior_panel, selected, place):
    count = selected.shape[0]
    wide, narrow = my_rows.shape[1], prior_panel.shape[1]
    return pl.pallas_call(
        pick_kernel,
        out_shape=[jax.ShapeDtypeStruct((count // 2, wide + narrow), BF16)] * 2,
        in_specs=[
            pl.BlockSpec(memory_space=pltpu.SMEM),
            pl.BlockSpec(memory_space=pltpu.SMEM),
            pl.BlockSpec(memory_space=pl.ANY),
            pl.BlockSpec(memory_space=pl.ANY),
        ],
        out_specs=[pl.BlockSpec(memory_space=pltpu.VMEM)] * 2,
        scratch_shapes=[
            pltpu.VMEM((count, 1 << TILE_BITS, wide), BF16),
            pltpu.VMEM((count, 1 << TILE_BITS, narrow), BF16),
            pltpu.VMEM((count, wide + narrow), F32),
            pltpu.SMEM((count,), jnp.int32),
            pltpu.SemaphoreType.DMA((2,)),
        ],
        compiler_params=pltpu.CompilerParams(vmem_limit_bytes=VMEM),
        cost_estimate=SMALL,
        name="pick_rows",
    )(place, selected, my_rows, prior_panel)


def place_matrix(mask, count, dtype):
    place = lax.broadcasted_iota(jnp.int32, (count, count), 0)
    column = lax.broadcasted_iota(jnp.int32, (count, count), 1)
    return jnp.where((column ^ mask) == place, 1.0, 0.0).astype(dtype)


def project_kernel(place_ref, weight_ref, inverse_ref, half_ref, other_ref, share_ref, project_ref, payload_ref):
    count = project_ref.shape[1]
    wide = half_ref.shape[1]

    def times(rows):
        return lax.dot_general(inverse_ref[0], rows, (((1,), (1,)), ((), ())), preferred_element_type=F32).astype(BF16)

    placed = jnp.concatenate([times(half_ref[...]), times(other_ref[...])], axis=1)
    project = jnp.dot(placed, place_matrix(place_ref[2], count, BF16), preferred_element_type=F32).astype(BF16)
    project_ref[...] = project
    payload_ref[:, :count] = weight_ref[0] * jnp.dot(share_ref[:, :wide], project, preferred_element_type=F32)
    payload_ref[:, count:] = share_ref[:, wide:].astype(F32)


def make_project(place, weight, inverse_blocks, half, other, share):
    wide = inverse_blocks.shape[1]
    count = 2 * half.shape[0]
    part = share.shape[0]
    vmem = pl.BlockSpec(memory_space=pltpu.VMEM)
    smem = pl.BlockSpec(memory_space=pltpu.SMEM)
    return pl.pallas_call(
        project_kernel,
        in_specs=[smem, smem, vmem, vmem, vmem, vmem],
        out_specs=[vmem, vmem],
        out_shape=[jax.ShapeDtypeStruct((wide, count), BF16), jax.ShapeDtypeStruct((part, 2 * count), F32)],
        compiler_params=pltpu.CompilerParams(vmem_limit_bytes=VMEM_SOME),
        cost_estimate=SMALL,
        name="make_project",
    )(place, weight, inverse_blocks, half, other, share)


def chunk_copies(lane, parts, ids_ref, border_ref, held, sem, got_refs, got_held, got_sems):
    step = held.shape[1]
    blocks = held.shape[0] // parts
    copies, got_copies = [], [[] for _ in got_refs]
    for j in range(parts):
        for t in range(blocks):
            slot = j * blocks + t
            source = border_ref.at[ids_ref[j], lane, pl.ds(t * step, step)]
            copies.append(pltpu.make_async_copy(source, held.at[slot], sem.at[slot]))
            for g, got_ref in enumerate(got_refs):
                source = got_ref.at[ids_ref[parts * (g + 1) + j], t]
                got_copies[g].append(pltpu.make_async_copy(source, got_held[g].at[slot], got_sems[g].at[slot]))
    for slot in range(len(copies)):
        copies[slot].start()
        for one in got_copies:
            one[slot].start()
    return copies, list(zip(got_copies, got_held))


def send_kernel(lane, parts, gots, ids_ref, border_ref, project_ref, weight_ref, *refs):
    got_refs, out_ref = refs[:gots], refs[gots]
    scratch = refs[gots + 1 :]
    held, sem, got_held, got_sems = scratch[0], scratch[1], scratch[2 : 2 + gots], scratch[2 + gots :]
    copies, incoming = chunk_copies(lane, parts, ids_ref, border_ref, held, sem, got_refs, got_held, got_sems)
    blocks = held.shape[0] // parts
    for slot in range(len(copies)):
        copies[slot].wait()
        total = jnp.dot(held[slot], project_ref[...], preferred_element_type=F32) * weight_ref[0]
        rows, cols = total.shape
        for got_copies, got in incoming:
            got_copies[slot].wait()
            power = got[slot, rows : rows + EXTRA, :].astype(F32)[0:1, :]
            total = total + got[slot, :rows, :].astype(F32) * jnp.exp2(power)
        largest = jnp.maximum(jnp.max(jnp.abs(total), axis=0, keepdims=True), 1e-30)
        power = jnp.ceil(jnp.log2(largest)) - 15.0
        whole = jnp.clip(jnp.round(total * jnp.exp2(-power)), -32767.0, 32767.0)
        out_ref[slot // blocks, slot % blocks, :rows, :] = whole.astype(jnp.int32).astype(jnp.int16)
        out_ref[slot // blocks, slot % blocks, rows:, :] = (
            jnp.broadcast_to(power, (EXTRA, cols)).astype(jnp.int32).astype(jnp.int16)
        )


def chunk_scratch(slots, step, wide, cols, gots):
    shapes = [pltpu.VMEM((slots, step, wide), BF16), pltpu.SemaphoreType.DMA((slots,))]
    shapes += [pltpu.VMEM((slots, step + EXTRA, cols), jnp.int16)] * gots
    return shapes + [pltpu.SemaphoreType.DMA((slots,))] * gots


def send_sum(border4, lane, ids, project, weight, gots):
    _, _, rows, wide = border4.shape
    cols = project.shape[1]
    parts = ids.shape[0] // (len(gots) + 1)
    step = min(rows, STEP)
    blocks = rows // step
    vmem = pl.BlockSpec(memory_space=pltpu.VMEM)
    smem = pl.BlockSpec(memory_space=pltpu.SMEM)
    hbm = pl.BlockSpec(memory_space=HBM)
    return pl.pallas_call(
        functools.partial(send_kernel, lane, parts, len(gots)),
        in_specs=[smem, hbm, vmem, smem] + [hbm] * len(gots),
        out_specs=vmem,
        out_shape=jax.ShapeDtypeStruct((parts, blocks, step + EXTRA, cols), jnp.int16),
        scratch_shapes=chunk_scratch(parts * blocks, step, wide, cols, len(gots)),
        compiler_params=pltpu.CompilerParams(vmem_limit_bytes=VMEM_SOME),
        cost_estimate=pl.CostEstimate(flops=1 << 16, bytes_accessed=12 << 20, transcendentals=0),
        name="send_sum",
    )(ids, border4, project, weight, *gots)


def factor_start(place_ref, half_ref, other_ref, work_ref, prior_ref):
    count = 2 * half_ref.shape[0]
    turn = place_matrix(place_ref[2], count, F32)

    def placed(columns):
        rows = jnp.concatenate([half_ref[:, columns], other_ref[:, columns]], axis=0)
        return lax.dot_general(turn, rows, (((0,), (0,)), ((), ())), preferred_element_type=F32, precision=EXACT)

    prior_sel = placed(slice(count, 2 * count)).astype(BF16)
    prior_ref[...] = prior_sel
    corner = placed(slice(0, count)) - lax.dot_general(
        prior_sel, prior_sel, (((1,), (1,)), ((), ())), preferred_element_type=F32
    )
    work_ref[:, :count] = 0.5 * (corner + corner.T)
    work_ref[:, count:] = jnp.where(
        lax.broadcasted_iota(jnp.int32, (count, count), 0) == lax.broadcasted_iota(jnp.int32, (count, count), 1), 1.0, 0.0
    )
    factor_blocks(work_ref, 0, 2)


def factor_finish(before_ref, high_ref, low_ref, work):
    count = before_ref.shape[0]
    work[...] = before_ref[...]
    factor_blocks(work, 2, 4)
    inverse = work[:, count:]
    top = inverse.astype(BF16)
    high_ref[...] = top
    low_ref[...] = (inverse - top.astype(F32)).astype(BF16)


def factor_blocks(work, begin, end):
    count = work.shape[0]
    side = count // 4
    for k in range(begin, end):
        low, high = k * side, (k + 1) * side
        same = jnp.where(
            lax.broadcasted_iota(jnp.int32, (side, side), 0) == lax.broadcasted_iota(jnp.int32, (side, side), 1), 1.0, 0.0
        )
        tiles = jnp.concatenate([work[low:high, low:high], same], axis=1)
        tiles = [tiles[8 * i : 8 * i + 8, :] for i in range(side // 8)]
        row_ids = lax.broadcasted_iota(jnp.int32, tiles[0].shape, 0)
        for j in range(0, side, PIVOTS):
            home, inner = j // 8, j % 8
            lanes = tiles[0].shape[1]
            columns = [
                [jnp.broadcast_to(tile[:, j + q : j + q + 1], tile.shape) for tile in tiles[home:]] for q in range(PIVOTS)
            ]
            rows = [tiles[home][inner + q : inner + q + 1, :] for q in range(PIVOTS)]
            for q in range(PIVOTS):
                pivot = columns[q][0][inner + q : inner + q + 1, :]
                scale = lax.rsqrt(pivot)
                scale = scale * (1.5 - 0.5 * pivot * scale * scale)
                rows[q] = rows[q] * scale
                columns[q] = [column * scale for column in columns[q]]
                for r in range(q + 1, PIVOTS):
                    entry = columns[q][0][inner + r : inner + r + 1, :]
                    rows[r] = rows[r] - entry * rows[q]
                    columns[r] = [a - entry * b for a, b in zip(columns[r], columns[q])]
            for i in range(home, side // 8):
                new = tiles[i]
                for q in range(PIVOTS):
                    new = new - columns[q][i - home] * rows[q]
                if i == home:
                    new = jnp.where(row_ids >= inner + PIVOTS, new, tiles[i])
                    for q in range(PIVOTS):
                        new = jnp.where(row_ids == inner + q, rows[q], new)
                tiles[i] = new
        inverse = jnp.concatenate([tile[:, side:] for tile in tiles], axis=0)
        block = jnp.dot(inverse, work[low:high, :], preferred_element_type=F32, precision=EXACT)
        work[low:high, :] = block
        if high < count:
            work[high:, :] = work[high:, :] - lax.dot_general(
                block[:, high:count], block, (((0,), (0,)), ((), ())), preferred_element_type=F32, precision=EXACT
            )

def factor_call(kernel, shapes, args, scratch=()):
    vmem = pl.BlockSpec(memory_space=pltpu.VMEM)
    smem = pl.BlockSpec(memory_space=pltpu.SMEM)
    return pl.pallas_call(
        kernel,
        in_specs=[smem if arg.ndim == 1 else vmem for arg in args],
        out_specs=[vmem] * len(shapes),
        out_shape=shapes,
        scratch_shapes=list(scratch),
        compiler_params=pltpu.CompilerParams(vmem_limit_bytes=VMEM_SOME),
        cost_estimate=SMALL,
        name=kernel.__name__,
    )(*args)


def start_factor(place, half, other):
    count = 2 * half.shape[0]
    shapes = [jax.ShapeDtypeStruct((count, 2 * count), F32), jax.ShapeDtypeStruct((count, count), BF16)]
    return factor_call(factor_start, shapes, [place, half, other])


def finish_factor(work):
    count = work.shape[0]
    shapes = [jax.ShapeDtypeStruct((count, count), BF16)] * 2
    return factor_call(factor_finish, shapes, [work], [pltpu.VMEM(work.shape, F32)])


def panel_kernel(lane, gots, aliased, ids_ref, border_ref, project_ref, weight_ref, *refs):
    got_refs, refs = refs[:gots], refs[gots:]
    first_ref, prior_ref, prior_sel_ref, high_ref, low_ref, sel_ref = refs[:6]
    out_ref, turned_ref = refs[6 + aliased : 8 + aliased]
    scratch = refs[8 + aliased :]
    held, sem, got_held, got_sems = scratch[0], scratch[1], scratch[2 : 2 + gots], scratch[2 + gots :]
    copies, incoming = chunk_copies(lane, 1, ids_ref, border_ref, held, sem, got_refs, got_held, got_sems)

    def times(a, b):
        return lax.dot_general(a, b, (((1,), (1,)), ((), ())), preferred_element_type=F32)

    for slot in range(len(copies)):
        rows = held.shape[1]
        here = slice(slot * rows, (slot + 1) * rows)
        copies[slot].wait()
        total = jnp.dot(held[slot], project_ref[...], preferred_element_type=F32) * weight_ref[0]
        total = total - times(prior_ref[here, :], prior_sel_ref[...])
        for got_copies, got in incoming:
            got_copies[slot].wait()
            power = got[slot, rows : rows + EXTRA, :].astype(F32)[0:1, :]
            total = total + got[slot, :rows, :].astype(F32) * jnp.exp2(power)
        high = total.astype(BF16)
        low = (total - high.astype(F32)).astype(BF16)
        solved = times(high, high_ref[...]) + (times(low, high_ref[...]) + times(high, low_ref[...]))
        ids = first_ref[0] + slot * rows + lax.broadcasted_iota(jnp.int32, (rows, 1), 0)
        hits = jnp.where(ids == sel_ref[0:1, :], 1.0, 0.0)
        marked = jnp.max(hits, axis=1, keepdims=True)
        solved = jnp.where(marked > 0.0, 0.0, solved)
        out_ref[here, :] = solved
        turned_ref[:, here] = jnp.transpose(solved.astype(BF16))


def panel_rows(border4, lane, ids, project, weight, gots, first, prior_panel, prior_sel, high, low, sel8, done):
    _, lanes, rows, wide = border4.shape
    own, cols = prior_panel.shape
    step = min(rows, STEP)
    vmem = pl.BlockSpec(memory_space=pltpu.VMEM)
    smem = pl.BlockSpec(memory_space=pltpu.SMEM)
    hbm = pl.BlockSpec(memory_space=HBM)
    mine = pl.BlockSpec((rows, cols), lambda t: (lane, 0))
    in_specs = [smem, hbm, vmem, smem] + [hbm] * len(gots) + [smem, mine, vmem, vmem, vmem, vmem]
    args = [ids, border4, project, weight, *gots, first, prior_panel, prior_sel, high, low, sel8]
    aliases = {}
    if done is not None:
        in_specs.append(hbm)
        args.append(done)
        aliases = {len(args) - 1: 0}
    return pl.pallas_call(
        functools.partial(panel_kernel, lane, len(gots), len(aliases)),
        grid=(1,),
        in_specs=in_specs,
        out_specs=[mine, vmem],
        out_shape=[jax.ShapeDtypeStruct((own, cols), F32), jax.ShapeDtypeStruct((cols, rows), BF16)],
        input_output_aliases=aliases,
        scratch_shapes=chunk_scratch(rows // step, step, wide, cols, len(gots)),
        compiler_params=pltpu.CompilerParams(vmem_limit_bytes=VMEM_SOME),
        cost_estimate=pl.CostEstimate(flops=1 << 16, bytes_accessed=16 << 20, transcendentals=0),
        name="panel_rows",
    )(*args)


def residual_kernel(lanes, ids_ref, border_ref, *refs):
    parts = len(lanes)
    pieces, out_ref, held, sems, turned, turned_sems = refs[:parts], *refs[-5:]
    before = None
    if len(refs) > parts + 5:
        before = pltpu.make_async_copy(refs[parts], out_ref, turned_sems.at[parts])
        before.start()
    members, _, block = out_ref.shape
    step = held.shape[1]
    blocks = turned.shape[2] // step
    copies, turned_copies = [], []
    for j in range(parts):
        turned_copies.append(pltpu.make_async_copy(pieces[j], turned.at[j], turned_sems.at[j]))
        turned_copies[j].start()
        for t in range(blocks):
            slot = j * blocks + t
            source = border_ref.at[ids_ref[j], lanes[j], pl.ds(t * step, step)]
            copies.append(pltpu.make_async_copy(source, held.at[slot], sems.at[slot]))
            copies[slot].start()
    for slot, copy in enumerate(copies):
        j, t = slot // blocks, slot % blocks
        if t == 0:
            turned_copies[j].wait()
        copy.wait()
        if slot == 0 and before is not None:
            before.wait()
        product = jnp.dot(turned[j][:, t * step : (t + 1) * step], held[slot], preferred_element_type=F32)
        for m in range(members):
            here = product[:, m * block : (m + 1) * block]
            if slot > 0 or before is not None:
                out_ref[m] += here
            else:
                out_ref[m] = here


def residual_add(border4, members, pieces, total):
    _, _, rows, wide = border4.shape
    cols = pieces[0][0].shape[0]
    parts = len(pieces)
    step = min(rows, STEP)
    slots = parts * (rows // step)
    ids = jnp.stack([at for _, at, _ in pieces]).astype(jnp.int32)
    vmem = pl.BlockSpec(memory_space=pltpu.VMEM)
    args = [ids, border4] + [block for block, _, _ in pieces]
    if total is not None:
        args.append(total)
    return pl.pallas_call(
        functools.partial(residual_kernel, [lane for _, _, lane in pieces]),
        in_specs=[pl.BlockSpec(memory_space=pltpu.SMEM)] + [pl.BlockSpec(memory_space=HBM)] * (len(args) - 1),
        out_specs=vmem,
        out_shape=jax.ShapeDtypeStruct((members, cols, wide // members), F32),
        scratch_shapes=[
            pltpu.VMEM((slots, step, wide), BF16),
            pltpu.SemaphoreType.DMA((slots,)),
            pltpu.VMEM((parts, cols, rows), BF16),
            pltpu.SemaphoreType.DMA((parts + 1,)),
        ],
        compiler_params=pltpu.CompilerParams(vmem_limit_bytes=VMEM_SOME),
        cost_estimate=pl.CostEstimate(flops=1 << 16, bytes_accessed=12 << 20, transcendentals=0),
        name="residual_add",
    )(*args)


def code_kernel(kept_ref, got_ref, sum_ref, coded_ref):
    rows, cols = kept_ref.shape[1:]
    for chip in range(kept_ref.shape[0]):
        total = kept_ref[chip] + got_ref[chip]
        sum_ref[chip] = total
        largest = jnp.maximum(jnp.max(jnp.abs(total), axis=0, keepdims=True), 1e-30)
        power = jnp.ceil(jnp.log2(largest)) - 15.0
        whole = jnp.clip(jnp.round(total * jnp.exp2(-power)), -32767.0, 32767.0)
        coded_ref[chip, :rows, :] = whole.astype(jnp.int32).astype(jnp.int16)
        coded_ref[chip, rows:, :] = jnp.broadcast_to(power, (EXTRA, cols)).astype(jnp.int32).astype(jnp.int16)


def code_sum(kept, got):
    chips, rows, cols = kept.shape
    vmem = pl.BlockSpec(memory_space=pltpu.VMEM)
    return pl.pallas_call(
        code_kernel,
        in_specs=[vmem, vmem],
        out_specs=[vmem, vmem],
        out_shape=[
            jax.ShapeDtypeStruct((chips, rows, cols), F32),
            jax.ShapeDtypeStruct((chips, rows + EXTRA, cols), jnp.int16),
        ],
        compiler_params=pltpu.CompilerParams(vmem_limit_bytes=VMEM_SOME),
        cost_estimate=SMALL,
        name="code_sum",
    )(kept, got)


def body(border, inverse_blocks, selected, assignment, probability, prior_panel):
    groups = lax.axis_size("grp")
    members = lax.axis_size("dev")
    group_index = lax.axis_index("grp")
    member = lax.axis_index("dev")
    group_bits = groups.bit_length() - 1
    member_bits = members.bit_length() - 1
    my_rows = border[0]
    height, wide = my_rows.shape
    own_rows, cols = prior_panel.shape
    lanes = min(LANES, own_rows // 128)
    lane_rows = own_rows // lanes
    border4 = my_rows.reshape(groups, lanes, lane_rows, wide)
    first_row = (member * groups + group_index) * own_rows

    rank_list = jnp.arange(groups, dtype=jnp.int32)
    scenario = jnp.sum(jnp.where(rank_list == group_index, assignment, 0))
    weight = jnp.sum(jnp.where(rank_list == scenario, probability, 0.0))

    chips = members // 2
    part = selected.shape[0] // members
    mask = bit_of(member, 0) * (selected.shape[0] // 2) + (member >> 1) * part
    place = jnp.stack([member * height, first_row, mask]).astype(jnp.int32)

    def to_chip(block, shift):
        return lax.ppermute(block, "dev", [(i, i ^ (shift << 1)) for i in range(members)])

    def gather_chips(block):
        return jnp.concatenate([block] + [to_chip(block, shift) for shift in range(1, chips)], axis=0)

    keep, away = pick_rows(my_rows, prior_panel, selected, place)
    held = keep + swap(away, "dev", members, 0)
    got = [to_chip(held[shift * part : (shift + 1) * part], shift) for shift in range(1, chips)]
    share = functools.reduce(jnp.add, got, held[:part])
    half = gather_chips(share[:, :wide])
    other = swap(half, "dev", members, 0)
    weight = weight.reshape(1)
    project, summed = make_project(place, weight, inverse_blocks, half, other, share)
    sel8 = jnp.broadcast_to(selected[None, :], (8, selected.shape[0]))

    def orders(lane):
        shift = lane % group_bits
        return [(shift + i) % group_bits for i in range(group_bits)]

    def listing(order, done, flip):
        fixed = group_index ^ (flip << order[done]) if flip else group_index
        settled = done + 1 if flip else done
        free = order[settled:]
        found = []
        for j in range(1 << len(free)):
            value = fixed
            for i, bit in enumerate(free):
                value = (value & ~(1 << bit)) | (((j >> (len(free) - 1 - i)) & 1) << bit)
            found.append(value)
        return found

    def quarter_place(order, settled, quarter):
        index = 0
        for bit in order[settled:]:
            index = 2 * index + bit_of(quarter, bit)
        return index

    def stage_ids(order, stage):
        quarters = listing(order, stage, 1) if stage < group_bits else [group_index]
        ids = list(quarters)
        for earlier in range(stage):
            ids += [quarter_place(order, earlier + 1, quarter) for quarter in quarters]
        return jnp.stack([jnp.asarray(at, jnp.int32) for at in ids])

    gots = [[] for _ in range(lanes)]

    def send_stage(lane, stage, token, held_back=None):
        order = orders(lane)
        ids = after(stage_ids(order, stage), token)
        sent = send_sum(border4, lane, ids, project, weight, gots[lane])
        if held_back is not None:
            sent = after(sent, held_back)
        gots[lane].append(swap(sent, "grp", groups, order[stage]))
        return sent

    def over_group(bit):
        return lambda rows: rows + swap(rows, "grp", groups, bit)

    def over_chips(bit):
        return lambda rows: jnp.concatenate([rows, to_chip(rows, 1 << bit)], axis=0)

    steps = [over_group(bit) for bit in range(group_bits)] + [over_chips(bit) for bit in range(member_bits - 1)]
    token = project
    for lane in range(lanes):
        if lane < len(steps):
            summed = steps[lane](after(summed, token))
        token = send_stage(lane, 0, token, [summed] + ([gots[0][0]] if lane == lanes - 1 > 0 else []))
    for step in steps[lanes:]:
        summed = step(summed)
    corner_half = after(summed, token)
    line = list(range(lanes))
    line[:2] = line[1::-1]
    token = [token, gots[lanes > 1][0]]
    half_way = min(2, lanes)
    for stage in range(1, group_bits):
        for lane in line[:half_way]:
            token = send_stage(lane, stage, token)
            if lane == line[0]:
                corner_half = after(corner_half, token)
    corner_other = swap(corner_half, "dev", members, 0)
    work, prior_sel = start_factor(place, corner_half, after(corner_other, token))
    token = prior_sel
    for stage in range(1, group_bits):
        for lane in line[half_way:]:
            token = send_stage(lane, stage, token)
    inverse_high, inverse_low = finish_factor(after(work, token))
    token = inverse_high
    line = [lane ^ 1 for lane in range(lanes)] if lanes % 2 == 0 else line

    panel_out, early, pending = None, None, []
    near, far = [None] * lanes, [None] * lanes

    def panel_stage(lane, before, held_back, meanwhile=None):
        order = orders(lane)
        first = (first_row + lane * lane_rows).reshape(1).astype(jnp.int32)
        ids = after(stage_ids(order, group_bits), before)
        out, turned = panel_rows(
            border4, lane, ids, project, weight, gots[lane], first,
            prior_panel, prior_sel, inverse_high, inverse_low, sel8, panel_out,
        )
        if meanwhile is not None:
            held_back = held_back + [meanwhile(turned)]
        turned = after(turned, held_back)
        near[lane] = [(turned, group_index, lane)]
        for bit in order:
            near[lane].append((swap(turned, "grp", groups, bit), group_index ^ (1 << bit), lane))
        return out, turned

    def forward(lane, before=()):
        order = orders(lane)
        far[lane] = []
        layer = [((after(block, before), at, lane), i) for i, (block, at, _) in enumerate(near[lane][1:])]
        while layer:
            following = []
            for (block, at, _), i in layer:
                for k in range(i + 1, len(order)):
                    piece = (swap(block, "grp", groups, order[k]), at ^ (1 << order[k]), lane)
                    far[lane].append(piece)
                    following.append((piece, k))
            layer = following

    def blocks_of(pieces):
        return [block for block, _, _ in pieces]

    def add_up(pieces, before, total):
        return residual_add(border4, members, [(after(block, before), at, lane) for block, at, lane in pieces], total)

    def arrived(lane):
        return blocks_of(near[lane][1:])

    for turn, lane in enumerate(line):
        before, held_back, meanwhile = [token], [], None
        if turn == 1:
            held_back = [gots[other][-1] for other in line[2:]]
        if turn == 2:
            held_back = arrived(line[0])

            def meanwhile(raw):
                forward(line[0], raw)
                return raw

        if turn >= 3:
            before = before + arrived(line[turn - 2])
            forward(line[turn - 2])
            held_back = arrived(line[turn - 1]) + blocks_of(far[line[turn - 3]] + far[line[turn - 2]])

            def meanwhile(raw):
                nonlocal early
                early = add_up(near[line[turn - 2]], raw, early)
                return early

        panel_out, token = panel_stage(lane, before, held_back, meanwhile)
        if turn == 2:
            early = add_up(near[line[0]], token, early)
            token = early
    forward(line[-2])
    early = add_up([piece for lane in line[:-2] for piece in far[lane]] + near[line[-2]], token, early)
    forward(line[-1], early)
    early = add_up(near[line[-1]], early, early)
    total = residual_add(border4, members, far[line[-2]] + far[line[-1]], early)

    core, chip = bit_of(member, 0), member >> 1

    def sum_cores(total):
        held = total.reshape((chips, 2) + total.shape[1:])
        away = lax.dynamic_index_in_dim(held, 1 - core, 1, keepdims=False)
        return lax.dynamic_index_in_dim(held, core, 1, keepdims=False), swap(away, "dev", members, 0)

    def sum_chips(held):
        return [to_chip(lax.dynamic_index_in_dim(held, chip ^ shift, 0, keepdims=False), shift) for shift in range(1, chips)]

    held, coded = code_sum(*sum_cores(total))
    result = lax.dynamic_index_in_dim(held, chip, 0, keepdims=False)
    for got in sum_chips(coded):
        result = result + got[:cols].astype(F32) * jnp.exp2(got[cols : cols + 1].astype(F32))
    residual = result.T / math.sqrt(N1)
    return (panel_out, residual[None])


def solution(mesh):
    return jax.shard_map(
        body,
        mesh=mesh,
        in_specs=(
            P("grp", "dev", None),
            P("grp", None, None),
            P(),
            P(),
            P(),
            P(("dev", "grp"), None),
        ),
        out_specs=(P(("dev", "grp"), None), P("grp", "dev", None)),
        check_vma=False,
    )
```
